128 devices in a mesh: inst: 32 (over z, y, x_hi), head: 4 (over x_lo, core).
Axes of the slice: x: 4 (x_hi: 2, x_lo: 2; x = x_hi * 2 + x_lo), y: 4, z: 4, core: 2. Of those that a mesh axis runs over, the one named last changes fastest.
Arguments:
- queries: bfloat16 [8192, 32, 128], P('inst', 'head'), may hold values from -120 to 120
- keys: bfloat16 [8192, 4, 128], P('inst', 'head'), may hold values from -6 to 6
- values: bfloat16 [8192, 4, 128], P('inst', 'head'), may hold values from -6 to 6
- lengths: int32 [4], replicated, may hold values from 1 to 5120, 8192 in all
- prior_kv: bfloat16 [16384, 4, 256], P('inst', 'head'), may hold values from -6 to 6
- routes: int32 [1024, 1], P('inst'), may hold values from 0 to 31; in each aligned block of 32 rows (0 to 31, 32 to 63, ...) at most 2 rows name the same one
- out_weight: bfloat16 [4096, 4096], P('head'), may hold values from -0.09375 to 0.09375
Outputs:
- projected: bfloat16 [8192, 4096], P(('inst', 'head'))
- migrated: bfloat16 [2048, 16, 4, 256], P('inst', None, 'head')
The draws below stay inside these ranges and needn't reach their ends.
Inputs may be any that keep to these rules, and one draw needn't show every extreme that they name: The 4 lengths sum to 8192; the longest is exactly 5120. `routes`: among the 32 blocks of one source shard no target is named more than 2 times, and some source names some target exactly 2 times.
All inputs are finite; a program needn't handle non-finite values.
Results may differ from the reference program's by a relative error of at most 0.013.
Values may be sent and summed in bfloat16 or wider, within the bound.
A program may use at most 192 MiB of HBM per device.

```python
import math
import jax
import jax.numpy as jnp
import numpy as np
from jax import lax

KV_HEADS = 4
GROUP = 8
HEAD_DIM = 128
OUT = 4096
REQS = 4
BLOCK = 16
QH = 32
TOKENS = 8192
LMAX = 5120
BLK_DEV = 32
MOST = 2
N_INST = 32
N_HEAD = 4


def shared_keys(key):
    base_draw = jax.random.normal(key, (TOKENS, KV_HEADS, HEAD_DIM), jnp.float32)
    return jnp.clip(base_draw, -6.0, 6.0)


def draw_keys(key, part):
    base_draw = shared_keys(key)
    return base_draw.astype(jnp.bfloat16)


def draw_queries(key, part):
    key = jax.random.fold_in(key, 5)
    base_draw = 2.0 * jnp.clip(jax.random.normal(key, (TOKENS, QH, HEAD_DIM), jnp.float32), -6.0, 6.0)
    return base_draw.astype(jnp.bfloat16)


def block_scale(own_key, dims, split, low, largest):
    gain, own = 1.0, jax.random.fold_in(own_key, 6)
    for dim, parts in split:
        steps = jnp.exp(jax.random.uniform(jax.random.fold_in(own, dim), (parts,), jnp.float32, low / len(split), largest / len(split)))
        gain = gain * jnp.repeat(steps, dims[dim] // parts).reshape([-1 if axis == dim else 1 for axis in range(len(dims))])
    return gain


def profile(count, total, bound, skew):
    portions = [(1 << 20) // math.isqrt(standing ** skew) + 1 for standing in range(2, count + 1)]
    spare, counts = total - bound - (count - 1), [1] * (count - 1)
    while spare > 0:
        movable = [i for i in range(count - 1) if counts[i] < bound]
        whole, budget = sum([portions[i] for i in movable]), spare
        for i in movable:
            more = min(bound - counts[i], max(1, budget * portions[i] // whole), spare)
            counts[i] = counts[i] + more
            spare = spare - more
    return np.array([bound] + counts)


def uneven_parts(key, number_of, total, limit, skew):
    if number_of == 2:
        one = jax.random.randint(key, (), max(1, total - limit), min(limit, total - 1) + 1)
        return jnp.stack([one, total - one])
    tallies = jnp.asarray(profile(number_of, total, limit, skew), jnp.int32)
    pairs = (number_of - 1) // 2
    source_of, taker = tallies[1:1 + 2 * pairs:2], tallies[2:2 + 2 * pairs:2]
    room = jnp.minimum(source_of - 1, limit - taker)
    passed = jax.random.randint(jax.random.fold_in(key, 1), (pairs,), 0, 1 << 20) % (room + 1)
    tallies = tallies.at[1:1 + 2 * pairs:2].set(source_of - passed).at[2:2 + 2 * pairs:2].set(taker + passed)
    return tallies[jax.random.permutation(jax.random.fold_in(key, 2), number_of)]


def shared_out(key, own, number, rows, amount, top, most, lean):
    sequence = jax.random.permutation(key, amount)
    crowded, usual = load_shares(amount, rows * top, most, lean, True), load_shares(amount, rows * top, most, lean, False)
    places = jnp.arange(amount)

    def named(sizes, rotation):
        used = int((sizes > 0).sum())
        fixed = max(1, used // 4)
        shifted = fixed + (places - fixed + rotation * (used - fixed)) % max(1, amount - fixed)
        return jnp.zeros((amount,), jnp.int32).at[sequence[jnp.where(places < fixed, places, shifted)]].set(jnp.asarray(sizes, jnp.int32))

    sizes = jnp.where(number % 4 == 0, named(crowded, number // 4), named(usual, number - number // 4 - 1))
    mixed = jax.random.permutation(jax.random.fold_in(own, 3), amount)
    source_of, sink = mixed[0:amount // 2 * 2:2], mixed[1:amount // 2 * 2:2]
    room = jnp.minimum(sizes[source_of] - 1, most - sizes[sink]) // 2
    room = jnp.where((source_of == sequence[0]) | (sink == sequence[0]) | (sizes[sink] == 0), 0, jnp.maximum(room, 0))
    shifted = jax.random.randint(jax.random.fold_in(own, 4), (amount // 2,), 0, 1 << 20) % (room + 1)
    sizes = sizes.at[source_of].add(-shifted).at[sink].add(shifted)
    labels = jnp.searchsorted(jnp.cumsum(sizes), jnp.arange(rows * top), side="right").astype(jnp.int32)
    listing = labels.reshape(top, rows).T
    listing = listing[jax.random.permutation(jax.random.fold_in(own, 1), rows)]
    rotation = jax.random.randint(jax.random.fold_in(own, 2), (rows, 1), 0, top)
    return jnp.take_along_axis(listing, (jnp.arange(top)[None, :] + rotation) % top, axis=1)


def load_shares(number_of, total, most, skew, full):
    loads = [(1 << 20) // math.isqrt(standing ** skew) + 1 for standing in range(1, number_of + 1)]
    largest = most if full else min(most, max(-(-total // number_of), total * loads[0] // sum(loads)))
    least = 1 if total - largest >= number_of - 1 else 0
    holding, spare = [largest] + [least] * (number_of - 1), total - largest - least * (number_of - 1)
    while spare > 0:
        movable = [i for i in range(1, number_of) if holding[i] < largest] or [i for i in range(1, number_of) if holding[i] < most]
        whole, left = sum([loads[i] for i in movable]), spare
        for i in movable:
            extra = min(most - holding[i], max(1, left * loads[i] // whole), spare)
            holding[i] = holding[i] + extra
            spare = spare - extra
    return np.array(holding)


def scatter_about(key, shape, spread, bound, cuts=(), held_as=jnp.bfloat16):
    factor_of = block_scale(key, shape, cuts, -0.22, 0.18) if cuts else 1.0
    array = jax.random.normal(key, shape, jnp.float32) * spread * factor_of
    return jnp.minimum(jnp.maximum(array, -bound), bound).astype(held_as)


def setup_inputs(seed: int = 0) -> dict:
    arg_keys = jax.random.split(jax.random.key(seed), 8)
    queries = draw_queries(jax.random.fold_in(arg_keys[7], 71), 0)
    keys = draw_keys(jax.random.fold_in(arg_keys[7], 71), 0)
    values = scatter_about(arg_keys[2], (TOKENS, KV_HEADS, HEAD_DIM), 1.0, 6.0, ((0, 32), (1, 4)))
    lengths = uneven_parts(arg_keys[3], REQS, TOKENS, LMAX, 2).astype(jnp.int32)
    prior_kv = scatter_about(arg_keys[4], (2 * TOKENS, KV_HEADS, 2 * HEAD_DIM), 1.0, 6.0, ((0, 32), (1, 4)))
    routes_keys = jax.random.split(jax.random.fold_in(arg_keys[5], 1), (N_INST * BLK_DEV) // BLK_DEV)
    routes_turns = jax.random.permutation(jax.random.fold_in(arg_keys[5], 3), (N_INST * BLK_DEV) // BLK_DEV)
    routes = jax.vmap(lambda own, number: shared_out(jax.random.fold_in(arg_keys[5], 2), own, number, BLK_DEV, N_INST, 1, MOST, 2))(routes_keys, routes_turns).reshape((N_INST * BLK_DEV, 1))
    out_weight = scatter_about(arg_keys[6], (QH * HEAD_DIM, OUT), (QH * HEAD_DIM) ** -0.5, 0.09375, ((0, 4),))
    return {"queries": queries, "keys": keys, "values": values, "lengths": lengths, "prior_kv": prior_kv, "routes": routes, "out_weight": out_weight}


def reference(queries, keys, values, lengths, prior_kv, routes, out_weight):
    doc_ends = jnp.cumsum(lengths)
    positions = jnp.arange(TOKENS, dtype=jnp.int32)
    doc_ids = lax.optimization_barrier(jnp.sum((positions[:, None] >= doc_ends[None, :]).astype(jnp.int32), axis=1))
    key_float = keys.astype(jnp.float32)
    value_float = values.astype(jnp.float32)
    score_scale = 1.0 / math.sqrt(HEAD_DIM)
    row_count = math.gcd(TOKENS, 128)

    def one_block(block_index):
        first_row = (block_index * row_count).astype(jnp.int32)
        query_part = lax.dynamic_slice_in_dim(queries, first_row, row_count, 0).astype(jnp.float32)
        query_part = query_part.reshape(row_count, KV_HEADS, GROUP, HEAD_DIM)
        query_pos = first_row + jnp.arange(row_count, dtype=jnp.int32)
        query_doc = lax.dynamic_slice_in_dim(doc_ids, first_row, row_count, 0)
        allowed = (positions[None, :] <= query_pos[:, None]) & (doc_ids[None, :] == query_doc[:, None])
        scores = jnp.einsum('qcgd,kcd->cgqk', query_part, key_float) * score_scale
        scores = jnp.where(allowed[None, None], scores, -1e+30)
        top_score = lax.optimization_barrier(jnp.max(scores, axis=-1, keepdims=True))
        weights = jnp.where(allowed[None, None], jnp.exp(scores - top_score), 0.0)
        totals = lax.optimization_barrier(jnp.sum(weights, axis=-1))
        rounded = weights.astype(jnp.bfloat16).astype(jnp.float32)
        blended = jnp.einsum('cgqk,kcd->qcgd', rounded, value_float)
        blended = blended / jnp.transpose(totals, (2, 0, 1))[..., None]
        return blended.reshape(row_count, QH * HEAD_DIM).astype(jnp.bfloat16)
    attended = lax.map(one_block, jnp.arange(TOKENS // row_count, dtype=jnp.int32))
    attended = attended.reshape(TOKENS, QH * HEAD_DIM)
    head_width = QH * HEAD_DIM // N_HEAD
    projected = jnp.zeros((TOKENS, OUT), jnp.float32)
    for group_index in range(N_HEAD):
        lower = group_index * head_width
        partial_term = jnp.dot(attended[:, lower:lower + head_width], out_weight[lower:lower + head_width], preferred_element_type=jnp.float32)
        projected = projected + partial_term.astype(jnp.bfloat16).astype(jnp.float32)
    projected = projected.astype(jnp.bfloat16)
    block_total = N_INST * BLK_DEV
    blocks = prior_kv.reshape(block_total, BLOCK, KV_HEADS, 2 * HEAD_DIM)
    target = routes[:, 0].reshape(N_INST, BLK_DEV)
    onehot = (target[:, :, None] == jnp.arange(N_INST, dtype=jnp.int32)[None, None, :]).astype(jnp.int32)
    ranks = lax.optimization_barrier(jnp.sum((jnp.cumsum(onehot, axis=1) - onehot) * onehot, axis=2))
    source = jnp.arange(N_INST, dtype=jnp.int32)[:, None]
    slot_index = (target * (N_INST * MOST) + source * MOST + ranks).reshape(block_total).astype(jnp.int32)
    migrated = jnp.zeros((N_INST * N_INST * MOST, BLOCK, KV_HEADS, 2 * HEAD_DIM), jnp.bfloat16)
    migrated = migrated.at[slot_index].set(blocks)
    return (projected, migrated)
```

```python
import functools
import math

import jax
import jax.numpy as jnp
from jax import lax
from jax.experimental import pallas as pl
from jax.experimental.pallas import tpu as pltpu
from jax.sharding import PartitionSpec as P

MESH = pl.DeviceIdType.MESH
F32, BF16 = jnp.float32, jnp.bfloat16
BLOCK = 16
TOK = 256
HEADS = 8
HD = 128
N_INST = 32
WINDOW = 20
GRP = 4
PAD = 4
PARTS = ((0, 96), (96, 48), (144, 112))
QROWS = 512
TILE = 256
CHUNKS = 4
CW = 1024
BIG = float(2 ** 30)
SCALE = math.log2(math.e) / math.sqrt(HD)


def doc_of(positions, ends):
    doc = jnp.zeros(positions.shape, jnp.int32)
    for e in ends:
        doc = doc + (positions >= e).astype(jnp.int32)
    return doc


def kernel(lengths, q_hbm, k_ref, v_ref, prior_hbm, rcol, rrow, w_hbm,
           out_ref, mig_ref,
           kv, feat, qraw, qf, qx, acc, mx, prior, outgoing, wbuf, att,
           keep, s1_out, s1_in, x_out, x_in, s2_out, s2_in,
           loc, ssem, rsem, msem, mrsem, rs_s, rs_r):
    me = lax.axis_index("inst")
    hd = lax.axis_index("head")
    z, r = me // 8, lax.rem(me, 8)
    y, h = r // 2, lax.rem(r, 2)
    xl, c = hd // 2, lax.rem(hd, 2)
    sib = (me, 2 * xl + 1 - c)
    across = (me, 2 * (1 - xl) + c)

    q_copy = pltpu.make_async_copy(q_hbm, qraw, loc.at[0])
    p_copy = pltpu.make_async_copy(prior_hbm, prior, loc.at[1])
    w_copy = pltpu.make_async_copy(w_hbm, wbuf, loc.at[2])
    q_copy.start()
    p_copy.start()
    w_copy.start()

    barrier = pltpu.get_barrier_semaphore()

    def greet(d, carry):
        pl.semaphore_signal(barrier, inc=1, device_id=(lax.rem(me + d, N_INST), hd), device_id_type=MESH)
        return carry

    lax.fori_loop(1, N_INST, greet, 0)
    pl.semaphore_signal(barrier, inc=1, device_id=sib, device_id_type=MESH)
    pl.semaphore_signal(barrier, inc=1, device_id=across, device_id_type=MESH)

    own = pl.multiple_of((me + PAD) * TOK, TOK)
    kv[pl.ds(own, TOK), :HD] = k_ref[...]
    kv[pl.ds(own, TOK), HD:] = v_ref[...]
    pl.semaphore_wait(barrier, N_INST + 1)

    def piece(part, blk):
        first, rows = PARTS[part]
        return kv.at[pl.ds(pl.multiple_of((blk + PAD) * TOK + first, 16), rows), :]

    def send(part, blk, target, slot):
        return pltpu.make_async_remote_copy(
            src_ref=piece(part, blk), dst_ref=piece(part, blk),
            send_sem=ssem.at[part, slot], recv_sem=rsem.at[part, blk],
            device_id=(target, hd), device_id_type=MESH)

    def arrive(part, blk):
        send(part, blk, me, 0).wait_recv()

    def z_first(part, act):
        def one(dz, carry):
            @pl.when((z + dz < 4) & ((dz < 3) | (r >= 4)))
            def _():
                act(send(part, me, me + 8 * dz, dz - 1))
            return carry
        lax.fori_loop(1, 4, one, 0)

    def p0_h(act):
        act(send(0, me, z * 8 + y * 2 + 1 - h, 0))

    def p0_y(act):
        def one(n, carry):
            y2 = lax.rem(y + 1 + n // 2, 4)
            act(send(0, z * 8 + y * 2 + lax.rem(n, 2), z * 8 + y2 * 2 + h, 1 + n))
            return carry
        lax.fori_loop(0, 6, one, 0)

    def needs(dst, src):
        return (dst - src >= 1) & (dst - src <= WINDOW)

    def p0_z(act):
        def one(n, carry):
            dz, src = 1 + n // 8, z * 8 + 7 - lax.rem(n, 8)
            dst = me + 8 * dz
            @pl.when((z + dz < 4) & needs(dst, src))
            def _():
                act(send(0, src, dst, 7 + n))
            return carry
        lax.fori_loop(0, 24, one, 0)

    def p1_h(act):
        def one(dz, carry):
            @pl.when((z >= dz) & ((dz < 3) | (r >= 4)))
            def _():
                act(send(1, me - 8 * dz, z * 8 + y * 2 + 1 - h, 3 + dz))
            return carry
        lax.fori_loop(0, 4, one, 0)

    def p1_y(act):
        def one(n, carry):
            dz = n // 6
            y2 = lax.rem(y + 1 + lax.rem(n, 6) // 2, 4)
            src = (z - dz) * 8 + y * 2 + lax.rem(n, 2)
            dst = z * 8 + y2 * 2 + h
            @pl.when((z >= dz) & needs(dst, src))
            def _():
                act(send(1, src, dst, 7 + n))
            return carry
        lax.fori_loop(0, 24, one, 0)

    def y_wants(dz, src_r, src_y, y2):
        return (((dz == 0) & (y2 > src_y)) | (dz == 1)
                | ((dz == 2) & (src_r >= 2 * y2 - 4)) | ((dz == 3) & (src_r >= 2 * y2 + 4)))

    def p2_y(act):
        def one(n, carry):
            dz = n // 3
            y2 = lax.rem(y + 1 + lax.rem(n, 3), 4)
            @pl.when((z >= dz) & y_wants(dz, r, y, y2))
            def _():
                act(send(2, me - 8 * dz, z * 8 + y2 * 2 + h, 3 + n))
            return carry
        lax.fori_loop(0, 12, one, 0)

    def p2_h(act):
        def one(n, carry):
            dz, y1 = n // 4, 3 - lax.rem(n, 4)
            src = (z - dz) * 8 + y1 * 2 + h
            dst = z * 8 + y * 2 + 1 - h
            @pl.when((z >= dz) & needs(dst, src))
            def _():
                act(send(2, src, dst, 15 + n))
            return carry
        lax.fori_loop(0, 16, one, 0)

    start = lambda copy: copy.start()
    done = lambda copy: copy.wait_send()

    p0_h(start)
    z_first(1, start)
    z_first(2, start)

    ends = []
    total = jnp.int32(0)
    for i in range(4):
        total = total + lengths[i]
        ends.append(total)
    kv[: PAD * TOK, :] = jnp.zeros((PAD * TOK, 2 * HD), BF16)

    def key_feature(b, carry):
        pos = (b - PAD) * TOK + lax.broadcasted_iota(jnp.int32, (TOK, HD), 0)
        lane = lax.broadcasted_iota(jnp.int32, (TOK, HD), 1)
        doc = jnp.where(pos < 0, 4, doc_of(pos, ends))
        feat[pl.ds(pl.multiple_of(b * TOK, TOK), TOK), :] = jnp.where(doc == lane, 1.0, 0.0).astype(BF16)
        return carry

    lax.fori_loop(0, N_INST + PAD, key_feature, 0)

    q_copy.wait()

    def widen(t, carry):
        rows = pl.ds(pl.multiple_of(t * TILE, TILE), TILE)
        qf[rows, :] = qraw[rows, :].astype(F32)
        return carry

    lax.fori_loop(0, 8, widen, 0)
    for quarter in range(4):
        pos = me * TOK + quarter * 64 + lax.broadcasted_iota(jnp.int32, (64, HD), 0)
        lane = lax.broadcasted_iota(jnp.int32, (64, HD), 1)
        doc = doc_of(pos, ends)
        mask = jnp.where((lane < 5) & (lane != doc), -BIG, 0.0).astype(BF16)
        for head in range(HEADS):
            rows = slice(quarter * QROWS + head * 64, quarter * QROWS + head * 64 + 64)
            qx[rows, :HD] = qf[pl.ds(quarter * QROWS + head, 64, stride=HEADS), :].astype(BF16)
            qx[rows, HD:] = mask

    arrive(0, z * 8 + y * 2 + 1 - h)
    p0_y(start)

    def columns(part):
        def one(dz, carry):
            @pl.when((z >= dz) & ((dz < 3) | (r >= 4)))
            def _():
                arrive(part, me - 8 * dz)
            return carry
        lax.fori_loop(1, 4, one, 0)

    columns(1)
    p1_h(start)
    columns(2)
    p2_y(start)

    def tiles(body, half, count):
        for t in range(count):
            body(pl.multiple_of(half * 1024 + t * TILE, TILE), t)

    ones = jnp.ones((TOK, HD), BF16)

    def diagonal(half, carry):
        def body(base, t):
            rows = pl.ds(base, TILE)
            k = jnp.concatenate([kv[pl.ds(own, TOK), :HD], feat[pl.ds(own, TOK), :]], axis=1)
            v = jnp.concatenate([kv[pl.ds(own, TOK), HD:], ones], axis=1)
            s = lax.dot_general(qx[rows, :], k, (((1,), (1,)), ((), ())), preferred_element_type=F32)
            tok = 128 * half + 64 * (t // 2) + lax.rem(lax.broadcasted_iota(jnp.int32, (TILE, TOK), 0), 64)
            s = jnp.where(lax.broadcasted_iota(jnp.int32, (TILE, TOK), 1) <= tok, s, -BIG)
            m = jnp.broadcast_to(jnp.max(s, axis=1, keepdims=True), (TILE, HD))
            p = jnp.concatenate(
                [jnp.exp2((s[:, j * HD:(j + 1) * HD] - m) * SCALE).astype(BF16) for j in range(TOK // HD)], axis=1)
            mx[rows, :] = m
            acc[rows, :] = jnp.dot(p, v, preferred_element_type=F32)
        tiles(body, half, 4)
        return carry

    lax.fori_loop(0, 2, diagonal, 0)

    def in_plane_p0(n, carry):
        y2 = lax.rem(y + 1 + n // 2, 4)
        arrive(0, z * 8 + y2 * 2 + lax.rem(n, 2))
        return carry

    lax.fori_loop(0, 6, in_plane_p0, 0)
    p0_z(start)

    def pair_p1(dz, carry):
        @pl.when((z >= dz) & ((dz < 3) | (r >= 4)))
        def _():
            arrive(1, (z - dz) * 8 + y * 2 + 1 - h)
        return carry

    lax.fori_loop(0, 4, pair_p1, 0)
    p1_y(start)

    def column_p2(n, carry):
        dz = n // 3
        y1 = lax.rem(y + 1 + lax.rem(n, 3), 4)
        r1 = y1 * 2 + h
        @pl.when((z >= dz) & y_wants(dz, r1, y1, y))
        def _():
            arrive(2, (z - dz) * 8 + r1)
        return carry

    lax.fori_loop(0, 12, column_p2, 0)
    p2_h(start)

    p_copy.wait()
    blk = lax.broadcasted_iota(jnp.int32, (32, 512), 0)
    col = lax.broadcasted_iota(jnp.int32, (32, 512), 1)
    target = jnp.broadcast_to(rrow[...], (32, 512))
    earlier = (jnp.broadcast_to(rcol[...], (32, 512)) == target) & (blk < col // BLOCK)
    rank = jnp.sum(earlier.astype(F32), axis=0, keepdims=True).astype(jnp.int32)
    code = rrow[...] * 32 + rank * BLOCK + lax.rem(col[:1], BLOCK)

    def place(t, carry):
        rows = t * TILE + lax.broadcasted_iota(jnp.int32, (TILE, 512), 0)
        hit = jnp.where(rows == jnp.broadcast_to(code, (TILE, 512)), 1.0, 0.0).astype(BF16)
        outgoing[pl.ds(pl.multiple_of(t * TILE, TILE), TILE), :] = jnp.dot(
            hit, prior[...], preferred_element_type=F32).astype(BF16)
        return carry

    lax.fori_loop(0, 4, place, 0)

    def slot_rows(ref, i):
        return ref.at[pl.ds(pl.multiple_of(i * 32, 32), 32), :]

    def migrate(d):
        there = lax.rem(me + d, N_INST)
        return pltpu.make_async_remote_copy(
            src_ref=slot_rows(outgoing, there), dst_ref=slot_rows(mig_ref, me),
            send_sem=msem.at[d], recv_sem=mrsem.at[d], device_id=(there, hd), device_id_type=MESH)

    stay = pltpu.make_async_copy(slot_rows(outgoing, me), slot_rows(mig_ref, me), loc.at[3])

    def collect(g):
        def one(n, carry):
            src = me - 1 - g * GRP - n
            zs, rs = src // 8, lax.rem(src, 8)
            @pl.when(src >= 0)
            def _():
                @pl.when(zs < z)
                def _():
                    arrive(0, src)
                @pl.when(rs // 2 != y)
                def _():
                    arrive(1, src)
                @pl.when(lax.rem(rs, 2) != h)
                def _():
                    arrive(2, src)
            return carry
        lax.fori_loop(0, GRP, one, 0)

    keys = GRP * TOK
    many = jnp.ones((keys, HD), BF16)

    def attend(g, first_tile, count):
        @pl.when(me - 1 - g * GRP >= 0)
        def _():
            ks = pl.ds(pl.multiple_of((me - g * GRP - GRP + PAD) * TOK, TOK), keys)
            for t in range(count):
                rows = pl.ds(pl.multiple_of(first_tile * TILE + t * TILE, TILE), TILE)
                k = jnp.concatenate([kv[ks, :HD], feat[ks, :]], axis=1)
                s = lax.dot_general(qx[rows, :], k, (((1,), (1,)), ((), ())), preferred_element_type=F32)
                old = mx[rows, :]
                m = jnp.maximum(old, jnp.max(s, axis=1, keepdims=True))
                shrink = jnp.exp2((old - m) * SCALE)
                mx[rows, :] = m
                p = jnp.concatenate(
                    [jnp.exp2((s[:, j * HD:(j + 1) * HD] - m) * SCALE).astype(BF16) for j in range(keys // HD)], axis=1)
                v = jnp.concatenate([kv[ks, HD:], many], axis=1)
                u = jnp.dot(p, v, preferred_element_type=F32)
                a = acc[rows, :]
                acc[rows, :] = jnp.concatenate([a[:, :HD] * shrink, a[:, HD:] * shrink], axis=1) + u

    def full_step(g, carry):
        collect(g)
        attend(g, 0, 8)
        return carry

    lax.fori_loop(0, 3, full_step, 0)

    def go(d, carry):
        migrate(d).start()
        return carry

    stay.start()
    lax.fori_loop(1, N_INST, go, 0)

    def half_step(base):
        def step(g, carry):
            attend(g, base, 4)
            return carry
        return step

    collect(3)
    collect(4)
    lax.fori_loop(3, 5, half_step((1 - xl) * 4), 0)

    def finish(half):
        for which in range(2):
            quarter = half * 2 + (1 - c if which == 0 else c)
            for head in range(HEADS):
                rows = pl.ds(pl.multiple_of(quarter * QROWS + head * 64, 64), 64)
                a = acc[rows, :]
                att[which * 64:(which + 1) * 64, head * HD:(head + 1) * HD] = (a[:, :HD] / a[:, HD:]).astype(BF16)

    def hop(src, dst, n, slot, target):
        return pltpu.make_async_remote_copy(
            src_ref=src.at[n], dst_ref=dst.at[n], send_sem=rs_s.at[slot, n], recv_sem=rs_r.at[slot, n],
            device_id=target, device_id_type=MESH)

    def project(n):
        return jnp.dot(att[...], wbuf[:, pl.ds(pl.multiple_of(n * CW, CW), CW)], preferred_element_type=F32)

    finish(1 - xl)
    w_copy.wait()

    def merge(n):
        hop(s1_out, s1_in, n, 0, sib).wait_recv()
        x_out[n] = (keep[n] + s1_in[n].astype(F32)).astype(BF16)
        hop(x_out, x_in, n, 1, across).start()

    def first_half(n, carry):
        p = project(n)
        s1_out[n] = p[:64].astype(BF16)
        hop(s1_out, s1_in, n, 0, sib).start()
        keep[n] = p[64:]
        @pl.when(n >= 1)
        def _():
            merge(n - 1)
        return carry

    lax.fori_loop(0, CHUNKS, first_half, 0)
    merge(CHUNKS - 1)

    lax.fori_loop(3, 5, half_step(xl * 4), 0)
    finish(xl)

    def second_half(n, carry):
        p = project(n)
        s2_out[n] = p[:64].astype(BF16)
        hop(s2_out, s2_in, n, 2, sib).start()
        keep[n] = p[64:]
        return carry

    lax.fori_loop(0, CHUNKS, second_half, 0)

    def last(n, carry):
        hop(s2_out, s2_in, n, 2, sib).wait_recv()
        hop(x_out, x_in, n, 1, across).wait_recv()
        out_ref[:, pl.ds(pl.multiple_of(n * CW, CW), CW)] = (
            keep[n] + s2_in[n].astype(F32) + x_in[n].astype(F32)).astype(BF16)
        return carry

    lax.fori_loop(0, CHUNKS, last, 0)

    p0_h(done)
    p0_y(done)
    p0_z(done)
    z_first(1, done)
    p1_h(done)
    p1_y(done)
    z_first(2, done)
    p2_y(done)
    p2_h(done)
    stay.wait()

    def gone(d, carry):
        migrate(d).wait()
        return carry

    lax.fori_loop(1, N_INST, gone, 0)

    def sent(n, carry):
        hop(s1_out, s1_in, n, 0, sib).wait_send()
        hop(x_out, x_in, n, 1, across).wait_send()
        hop(s2_out, s2_in, n, 2, sib).wait_send()
        return carry

    lax.fori_loop(0, CHUNKS, sent, 0)


def shards(queries, keys, values, lengths, prior_kv, routes, out_weight):
    rows = TOK * HEADS
    vmem = pl.BlockSpec(memory_space=pltpu.VMEM)
    hbm = pl.BlockSpec(memory_space=pl.ANY)
    blocks = (PAD + N_INST) * TOK
    quarter = (CHUNKS, 64, CW)
    projected, migrated = pl.pallas_call(
        kernel,
        out_shape=(
            jax.ShapeDtypeStruct((64, CHUNKS * CW), BF16),
            jax.ShapeDtypeStruct((N_INST * 2 * BLOCK, 2 * HD), BF16),
        ),
        in_specs=[pl.BlockSpec(memory_space=pltpu.SMEM), hbm, vmem, vmem, hbm, vmem, vmem, hbm],
        out_specs=(vmem, hbm),
        scratch_shapes=[
            pltpu.VMEM((blocks, 2 * HD), BF16),
            pltpu.VMEM((blocks, HD), BF16),
            pltpu.VMEM((rows, HD), BF16),
            pltpu.VMEM((rows, HD), F32),
            pltpu.VMEM((rows, 2 * HD), BF16),
            pltpu.VMEM((rows, 2 * HD), F32),
            pltpu.VMEM((rows, HD), F32),
            pltpu.VMEM((512, 2 * HD), BF16),
            pltpu.VMEM((1024, 2 * HD), BF16),
            pltpu.VMEM((HEADS * HD, CHUNKS * CW), BF16),
            pltpu.VMEM((128, HEADS * HD), BF16),
            pltpu.VMEM(quarter, F32),
            pltpu.VMEM(quarter, BF16),
            pltpu.VMEM(quarter, BF16),
            pltpu.VMEM(quarter, BF16),
            pltpu.VMEM(quarter, BF16),
            pltpu.VMEM(quarter, BF16),
            pltpu.VMEM(quarter, BF16),
            pltpu.SemaphoreType.DMA((4,)),
            pltpu.SemaphoreType.DMA((3, 32)),
            pltpu.SemaphoreType.DMA((3, 32)),
            pltpu.SemaphoreType.DMA((32,)),
            pltpu.SemaphoreType.DMA((32,)),
            pltpu.SemaphoreType.DMA((3, CHUNKS)),
            pltpu.SemaphoreType.DMA((3, CHUNKS)),
        ],
        compiler_params=pltpu.CompilerParams(
            collective_id=0, has_side_effects=True, vmem_limit_bytes=60 * 2 ** 20),
        name="attend_project_migrate",
    )(
        lengths,
        queries.reshape(rows, HD),
        keys.reshape(TOK, HD),
        values.reshape(TOK, HD),
        prior_kv.reshape(512, 2 * HD),
        routes,
        jnp.repeat(routes.reshape(1, 32), BLOCK, axis=1),
        out_weight,
    )
    return projected, migrated.reshape(64, BLOCK, 1, 2 * HD)


def solution(mesh):
    placed = (
        P("inst", "head", None),
        P("inst", "head", None),
        P("inst", "head", None),
        P(),
        P("inst", "head", None),
        P("inst", None),
        P("head", None),
    )
    return jax.shard_map(
        shards,
        mesh=mesh,
        in_specs=placed,
        out_specs=(P(("inst", "head"), None), P("inst", None, "head", None)),
        check_vma=False,
    )
```

```python
import functools
import math

import jax
import jax.numpy as jnp
from jax import lax
from jax.experimental import pallas as pl
from jax.experimental.pallas import tpu as pltpu
from jax.sharding import PartitionSpec as P

MESH = pl.DeviceIdType.MESH
F32, BF16 = jnp.float32, jnp.bfloat16
BLOCK = 16
TOK = 256
HEADS = 8
HD = 128
N_INST = 32
WINDOW = 20
GRP = 4
PAD = 4
PARTS = ((0, 96), (96, 48), (144, 112))
QROWS = 512
TILE = 256
CHUNKS = 4
CW = 1024
BIG = float(2 ** 30)
SCALE = math.log2(math.e) / math.sqrt(HD)


def doc_of(positions, ends):
    doc = jnp.zeros(positions.shape, jnp.int32)
    for e in ends:
        doc = doc + (positions >= e).astype(jnp.int32)
    return doc


def kernel(lengths, q_hbm, k_ref, v_ref, prior_hbm, routes, w_hbm,
           out_ref, mig_ref,
           kv, feat, qraw, qf, qx, acc, mx, prior, outgoing, wbuf, att,
           keep, s1_out, s1_in, x_out, x_in, s2_out, s2_in,
           loc, ssem, rsem, msem, mrsem, rs_s, rs_r):
    me = lax.axis_index("inst")
    hd = lax.axis_index("head")
    z, r = me // 8, lax.rem(me, 8)
    y, h = r // 2, lax.rem(r, 2)
    xl, c = hd // 2, lax.rem(hd, 2)
    sib = (me, 2 * xl + 1 - c)
    across = (me, 2 * (1 - xl) + c)

    q_copy = pltpu.make_async_copy(q_hbm, qraw, loc.at[0])
    p_copy = pltpu.make_async_copy(prior_hbm, prior, loc.at[1])
    w_copy = pltpu.make_async_copy(w_hbm, wbuf, loc.at[2])
    q_copy.start()
    p_copy.start()
    w_copy.start()

    barrier = pltpu.get_barrier_semaphore()

    def greet(d, carry):
        pl.semaphore_signal(barrier, inc=1, device_id=(lax.rem(me + d, N_INST), hd), device_id_type=MESH)
        return carry

    lax.fori_loop(1, N_INST, greet, 0)
    pl.semaphore_signal(barrier, inc=1, device_id=sib, device_id_type=MESH)
    pl.semaphore_signal(barrier, inc=1, device_id=across, device_id_type=MESH)

    own = pl.multiple_of((me + PAD) * TOK, TOK)
    kv[pl.ds(own, TOK), :HD] = k_ref[...]
    kv[pl.ds(own, TOK), HD:] = v_ref[...]
    pl.semaphore_wait(barrier, N_INST + 1)

    def piece(part, blk):
        first, rows = PARTS[part]
        return kv.at[pl.ds(pl.multiple_of((blk + PAD) * TOK + first, 16), rows), :]

    def send(part, blk, target, slot):
        return pltpu.make_async_remote_copy(
            src_ref=piece(part, blk), dst_ref=piece(part, blk),
            send_sem=ssem.at[part, slot], recv_sem=rsem.at[part, blk],
            device_id=(target, hd), device_id_type=MESH)

    def arrive(part, blk):
        send(part, blk, me, 0).wait_recv()

    def needs(dst, src):
        return (dst - src >= 1) & (dst - src <= WINDOW)

    def unroll(first, end, body):
        for n in range(first, end):
            body(n, 0)

    def wrap(v):
        return jnp.where(v >= 4, v - 4, v)

    def p0_h(act):
        act(send(0, me, z * 8 + y * 2 + 1 - h, 0))

    def p0_y(h1, slot, act):
        def one(n, carry):
            y2 = wrap(y + 1 + n)
            @pl.when((z < 3) | (y2 * 2 + h > y * 2 + h1))
            def _():
                act(send(0, z * 8 + y * 2 + h1, z * 8 + y2 * 2 + h, slot + n))
            return carry
        unroll(0, 3, one)

    def p0_z(r1, slot, act):
        def one(dz, carry):
            src, dst = z * 8 + r1, me + 8 * dz
            @pl.when((z + dz < 4) & needs(dst, src))
            def _():
                act(send(0, src, dst, slot + dz))
            return carry
        unroll(1, 4, one)

    def p0_rest(dz, act):
        def one(n, carry):
            src, dst = z * 8 + wrap(y + 1 + n // 2) * 2 + n % 2, me + 8 * dz
            @pl.when((z + dz < 4) & needs(dst, src))
            def _():
                act(send(0, src, dst, 16 + dz * 6 + n))
            return carry
        unroll(0, 6, one)

    def p0_plane():
        def one(n, carry):
            r1 = wrap(y + 1 + n // 2) * 2 + n % 2
            @pl.when((z < 3) | (r > r1))
            def _():
                arrive(0, z * 8 + r1)
            return carry
        unroll(0, 6, one)

    def column(dz):
        return (z >= dz) & ((dz < 3) | (r >= 4))

    def p12_z(part, act):
        def one(dz, carry):
            @pl.when((z + dz < 4) & ((dz < 3) | (r >= 4)))
            def _():
                act(send(part, me, me + 8 * dz, dz - 1))
            return carry
        unroll(1, 4, one)

    def p1_h(dz, act):
        @pl.when(column(dz))
        def _():
            act(send(1, me - 8 * dz, z * 8 + y * 2 + 1 - h, 3 + dz))

    def p1_y(dz, h1, slot, act):
        def one(n, carry):
            src, dst = (z - dz) * 8 + y * 2 + h1, z * 8 + wrap(y + 1 + n) * 2 + h
            @pl.when((z >= dz) & needs(dst, src))
            def _():
                act(send(1, src, dst, slot + 6 * dz + n))
            return carry
        unroll(0, 3, one)

    def y_wants(dz, r1, y1, y2):
        if dz == 0:
            return y2 > y1
        return (z >= dz) & ((dz == 1) | (r1 >= 2 * y2 + (4 if dz == 3 else -4)))

    def p2_y(dz, act):
        def one(n, carry):
            y2 = wrap(y + 1 + n)
            @pl.when(y_wants(dz, r, y, y2))
            def _():
                act(send(2, me - 8 * dz, z * 8 + y2 * 2 + h, 3 + dz * 3 + n))
            return carry
        unroll(0, 3, one)

    def p2_h(dz, first, count, slot, act):
        def one(n, carry):
            src = (z - dz) * 8 + wrap(y + first + n) * 2 + h
            dst = z * 8 + y * 2 + 1 - h
            @pl.when((z >= dz) & needs(dst, src))
            def _():
                act(send(2, src, dst, slot + dz * 4 + n))
            return carry
        unroll(0, count, one)

    def stage0(act):
        p0_h(act)
        p12_z(2, act)
        p12_z(1, act)
        p2_y(0, act)
        p0_y(h, 1, act)
        p1_h(0, act)
        p1_y(0, h, 8, act)
        p2_h(0, 0, 1, 16, act)
        p0_z(r, 6, act)

    def stage1(act, wait):
        if wait:
            arrive(0, z * 8 + y * 2 + 1 - h)
        p0_y(1 - h, 4, act)
        p0_z(y * 2 + 1 - h, 9, act)
        if wait:
            arrive(1, z * 8 + y * 2 + 1 - h)
        p1_y(0, 1 - h, 11, act)
        if wait:
            from_y(0)
        p2_h(0, 1, 3, 17, act)

    def from_y(dz):
        def one(n, carry):
            y1 = wrap(y + 1 + n)
            @pl.when(y_wants(dz, y1 * 2 + h, y1, y))
            def _():
                arrive(2, (z - dz) * 8 + y1 * 2 + h)
            return carry
        unroll(0, 3, one)

    def stage2(dz, act, wait):
        if wait:
            @pl.when(column(dz))
            def _():
                arrive(2, me - 8 * dz)
                arrive(1, me - 8 * dz)
        p2_y(dz, act)
        p1_h(dz, act)
        p1_y(dz, h, 8, act)
        p2_h(dz, 0, 1, 16, act)

    def stage3(act, wait):
        if wait:
            p0_plane()
        for dz in (1, 2, 3):
            p0_rest(dz, act)

    def stage4(dz, act, wait):
        if wait:
            @pl.when(column(dz))
            def _():
                arrive(1, (z - dz) * 8 + y * 2 + 1 - h)
        p1_y(dz, 1 - h, 11, act)
        if wait:
            from_y(dz)
        p2_h(dz, 1, 3, 17, act)

    start = lambda copy: copy.start()
    done = lambda copy: copy.wait_send()

    stage0(start)

    ends = []
    total = jnp.int32(0)
    for i in range(4):
        total = total + lengths[i]
        ends.append(total)
    kv[: PAD * TOK, :] = jnp.zeros((PAD * TOK, 2 * HD), BF16)

    def key_feature(b, carry):
        pos = (b - PAD) * TOK + lax.broadcasted_iota(jnp.int32, (TOK, HD), 0)
        lane = lax.broadcasted_iota(jnp.int32, (TOK, HD), 1)
        doc = jnp.where(pos < 0, 4, doc_of(pos, ends))
        feat[pl.ds(pl.multiple_of(b * TOK, TOK), TOK), :] = jnp.where(doc == lane, 1.0, 0.0).astype(BF16)
        return carry

    lax.fori_loop(0, N_INST + PAD, key_feature, 0)

    q_copy.wait()

    def widen(t, carry):
        rows = pl.ds(pl.multiple_of(t * TILE, TILE), TILE)
        qf[rows, :] = qraw[rows, :].astype(F32)
        return carry

    lax.fori_loop(0, 8, widen, 0)
    for quarter in range(4):
        pos = me * TOK + quarter * 64 + lax.broadcasted_iota(jnp.int32, (64, HD), 0)
        lane = lax.broadcasted_iota(jnp.int32, (64, HD), 1)
        doc = doc_of(pos, ends)
        mask = jnp.where((lane < 5) & (lane != doc), -BIG, 0.0).astype(BF16)
        for head in range(HEADS):
            rows = slice(quarter * QROWS + head * 64, quarter * QROWS + head * 64 + 64)
            qx[rows, :HD] = qf[pl.ds(quarter * QROWS + head, 64, stride=HEADS), :].astype(BF16)
            qx[rows, HD:] = mask

    def tiles(body, half, count):
        for t in range(count):
            body(pl.multiple_of(half * 1024 + t * TILE, TILE), t)

    ones = jnp.ones((TOK, HD), BF16)

    def diagonal(half, carry):
        def body(base, t):
            rows = pl.ds(base, TILE)
            k = jnp.concatenate([kv[pl.ds(own, TOK), :HD], feat[pl.ds(own, TOK), :]], axis=1)
            v = jnp.concatenate([kv[pl.ds(own, TOK), HD:], ones], axis=1)
            s = lax.dot_general(qx[rows, :], k, (((1,), (1,)), ((), ())), preferred_element_type=F32)
            tok = 128 * half + 64 * (t // 2) + lax.rem(lax.broadcasted_iota(jnp.int32, (TILE, TOK), 0), 64)
            s = jnp.where(lax.broadcasted_iota(jnp.int32, (TILE, TOK), 1) <= tok, s, -BIG)
            m = jnp.broadcast_to(jnp.max(s, axis=1, keepdims=True), (TILE, HD))
            p = jnp.concatenate(
                [jnp.exp2((s[:, j * HD:(j + 1) * HD] - m) * SCALE).astype(BF16) for j in range(TOK // HD)], axis=1)
            mx[rows, :] = m
            acc[rows, :] = jnp.dot(p, v, preferred_element_type=F32)
        tiles(body, half, 4)
        return carry


    def slot_rows(ref, i):
        return ref.at[pl.ds(pl.multiple_of(i * 32, 32), 32), :]

    def migrate(d):
        there = lax.rem(me + d, N_INST)
        return pltpu.make_async_remote_copy(
            src_ref=slot_rows(outgoing, there), dst_ref=slot_rows(mig_ref, me),
            send_sem=msem.at[d], recv_sem=mrsem.at[d], device_id=(there, hd), device_id_type=MESH)

    stay = pltpu.make_async_copy(slot_rows(outgoing, me), slot_rows(mig_ref, me), loc.at[3])

    def collect(g):
        def one(n, carry):
            src = me - 1 - g * GRP - n
            rs = lax.rem(src, 8)
            @pl.when(src >= 0)
            def _():
                @pl.when(src // 8 < z)
                def _():
                    arrive(0, src)
                @pl.when(rs // 2 != y)
                def _():
                    arrive(1, src)
                @pl.when(lax.rem(rs, 2) != h)
                def _():
                    arrive(2, src)
            return carry
        lax.fori_loop(0, GRP, one, 0)

    keys = GRP * TOK
    many = jnp.ones((keys, HD), BF16)

    def attend(g, first_tile, count):
        @pl.when(me - 1 - g * GRP >= 0)
        def _():
            ks = pl.ds(pl.multiple_of((me - g * GRP - GRP + PAD) * TOK, TOK), keys)
            for t in range(count):
                rows = pl.ds(pl.multiple_of(first_tile * TILE + t * TILE, TILE), TILE)
                k = jnp.concatenate([kv[ks, :HD], feat[ks, :]], axis=1)
                s = lax.dot_general(qx[rows, :], k, (((1,), (1,)), ((), ())), preferred_element_type=F32)
                old = mx[rows, :]
                m = jnp.maximum(old, jnp.max(s, axis=1, keepdims=True))
                shrink = jnp.exp2((old - m) * SCALE)
                mx[rows, :] = m
                p = jnp.concatenate(
                    [jnp.exp2((s[:, j * HD:(j + 1) * HD] - m) * SCALE).astype(BF16) for j in range(keys // HD)], axis=1)
                v = jnp.concatenate([kv[ks, HD:], many], axis=1)
                u = jnp.dot(p, v, preferred_element_type=F32)
                a = acc[rows, :]
                acc[rows, :] = jnp.concatenate([a[:, :HD] * shrink, a[:, HD:] * shrink], axis=1) + u

    def lay_out():
        p_copy.wait()
        row = lax.broadcasted_iota(jnp.int32, (32, 32), 0)
        lane = lax.broadcasted_iota(jnp.int32, (32, 32), 1)
        target = jnp.broadcast_to(routes[...], (32, 32))
        same = jnp.sum(jnp.where(row == lane, target, 0).astype(F32), axis=1, keepdims=True).astype(jnp.int32) == target
        rank = jnp.sum(jnp.where(same & (row < lane), 1.0, 0.0), axis=0, keepdims=True)
        slot = (2 * target[:8]).astype(F32) + jnp.broadcast_to(rank, (8, 32))
        blk = lax.broadcasted_iota(jnp.int32, (32, 512), 0)
        col = lax.broadcasted_iota(jnp.int32, (32, 512), 1)
        spread = jnp.where(blk == col // BLOCK, 1.0, 0.0).astype(BF16)
        slots = jnp.dot(slot.astype(BF16), spread, preferred_element_type=F32)
        code = (slots[:1].astype(jnp.int32)) * BLOCK + lax.rem(col[:1], BLOCK)

        def place(t, carry):
            rows = t * TILE + lax.broadcasted_iota(jnp.int32, (TILE, 512), 0)
            hit = jnp.where(rows == jnp.broadcast_to(code, (TILE, 512)), 1.0, 0.0).astype(BF16)
            outgoing[pl.ds(pl.multiple_of(t * TILE, TILE), TILE), :] = jnp.dot(
                hit, prior[...], preferred_element_type=F32).astype(BF16)
            return carry

        lax.fori_loop(0, 4, place, 0)

    def go(d, carry):
        migrate(d).start()
        return carry

    stage1(start, True)
    stage2(1, start, True)
    stage2(2, start, True)
    p0_plane()
    p0_rest(1, start)
    p0_rest(2, start)
    stage2(3, start, True)
    p0_rest(3, start)
    stage4(1, start, True)
    lax.fori_loop(0, 2, diagonal, 0)
    stage4(2, start, True)
    stage4(3, start, True)
    collect(0)
    attend(0, 0, 8)
    lay_out()
    collect(1)
    attend(1, 0, 8)
    stay.start()
    lax.fori_loop(1, N_INST, go, 0)
    collect(2)
    attend(2, (1 - xl) * 4, 4)
    collect(3)
    attend(3, (1 - xl) * 4, 4)
    collect(4)
    attend(4, (1 - xl) * 4, 4)

    def finish(half):
        for which in range(2):
            quarter = half * 2 + (1 - c if which == 0 else c)
            for head in range(HEADS):
                rows = pl.ds(pl.multiple_of(quarter * QROWS + head * 64, 64), 64)
                a = acc[rows, :]
                att[which * 64:(which + 1) * 64, head * HD:(head + 1) * HD] = (a[:, :HD] / a[:, HD:]).astype(BF16)

    def hop(src, dst, n, slot, target):
        return pltpu.make_async_remote_copy(
            src_ref=src.at[n], dst_ref=dst.at[n], send_sem=rs_s.at[slot, n], recv_sem=rs_r.at[slot, n],
            device_id=target, device_id_type=MESH)

    def project(n):
        return jnp.dot(att[...], wbuf[:, pl.ds(pl.multiple_of(n * CW, CW), CW)], preferred_element_type=F32)

    finish(1 - xl)
    w_copy.wait()

    def merge(n):
        hop(s1_out, s1_in, n, 0, sib).wait_recv()
        x_out[n] = (keep[n] + s1_in[n].astype(F32)).astype(BF16)
        hop(x_out, x_in, n, 1, across).start()

    def first_half(n, carry):
        p = project(n)
        s1_out[n] = p[:64].astype(BF16)
        hop(s1_out, s1_in, n, 0, sib).start()
        keep[n] = p[64:]
        @pl.when(n >= 1)
        def _():
            merge(n - 1)
        return carry

    lax.fori_loop(0, CHUNKS, first_half, 0)
    merge(CHUNKS - 1)

    attend(2, xl * 4, 4)
    attend(3, xl * 4, 4)
    attend(4, xl * 4, 4)

    finish(xl)

    def second_half(n, carry):
        p = project(n)
        s2_out[n] = p[:64].astype(BF16)
        hop(s2_out, s2_in, n, 2, sib).start()
        keep[n] = p[64:]
        return carry

    lax.fori_loop(0, CHUNKS, second_half, 0)

    stage0(done)
    stage1(done, False)
    stage3(done, False)
    for dz in (1, 2, 3):
        stage2(dz, done, False)
        stage4(dz, done, False)
    stay.wait()

    def gone(d, carry):
        migrate(d).wait()
        return carry

    lax.fori_loop(1, N_INST, gone, 0)

    def last(n, carry):
        hop(s2_out, s2_in, n, 2, sib).wait_recv()
        hop(x_out, x_in, n, 1, across).wait_recv()
        out_ref[:, pl.ds(pl.multiple_of(n * CW, CW), CW)] = (
            keep[n] + s2_in[n].astype(F32) + x_in[n].astype(F32)).astype(BF16)
        return carry

    lax.fori_loop(0, CHUNKS, last, 0)

    def sent(n, carry):
        hop(s1_out, s1_in, n, 0, sib).wait_send()
        hop(x_out, x_in, n, 1, across).wait_send()
        hop(s2_out, s2_in, n, 2, sib).wait_send()
        return carry

    lax.fori_loop(0, CHUNKS, sent, 0)


def hand_over(a, b, a_out, b_out, sem):
    first = pltpu.make_async_copy(a, a_out, sem.at[0])
    second = pltpu.make_async_copy(b, b_out, sem.at[1])
    first.start()
    second.start()
    first.wait()
    second.wait()


def shards(queries, keys, values, lengths, prior_kv, routes, out_weight):
    rows = TOK * HEADS
    vmem = pl.BlockSpec(memory_space=pltpu.VMEM)
    hbm = pl.BlockSpec(memory_space=pl.ANY)
    blocks = (PAD + N_INST) * TOK
    quarter = (CHUNKS, 64, CW)
    projected, migrated = pl.pallas_call(
        kernel,
        out_shape=(
            jax.ShapeDtypeStruct((64, CHUNKS * CW), BF16),
            jax.ShapeDtypeStruct((N_INST * 2 * BLOCK, 2 * HD), BF16),
        ),
        in_specs=[pl.BlockSpec(memory_space=pltpu.SMEM), hbm, vmem, vmem, hbm, vmem, hbm],
        out_specs=(vmem, hbm),
        scratch_shapes=[
            pltpu.VMEM((blocks, 2 * HD), BF16),
            pltpu.VMEM((blocks, HD), BF16),
            pltpu.VMEM((rows, HD), BF16),
            pltpu.VMEM((rows, HD), F32),
            pltpu.VMEM((rows, 2 * HD), BF16),
            pltpu.VMEM((rows, 2 * HD), F32),
            pltpu.VMEM((rows, HD), F32),
            pltpu.VMEM((512, 2 * HD), BF16),
            pltpu.VMEM((1024, 2 * HD), BF16),
            pltpu.VMEM((HEADS * HD, CHUNKS * CW), BF16),
            pltpu.VMEM((128, HEADS * HD), BF16),
            pltpu.VMEM(quarter, F32),
            pltpu.VMEM(quarter, BF16),
            pltpu.VMEM(quarter, BF16),
            pltpu.VMEM(quarter, BF16),
            pltpu.VMEM(quarter, BF16),
            pltpu.VMEM(quarter, BF16),
            pltpu.VMEM(quarter, BF16),
            pltpu.SemaphoreType.DMA((4,)),
            pltpu.SemaphoreType.DMA((3, 48)),
            pltpu.SemaphoreType.DMA((3, 48)),
            pltpu.SemaphoreType.DMA((32,)),
            pltpu.SemaphoreType.DMA((32,)),
            pltpu.SemaphoreType.DMA((3, CHUNKS)),
            pltpu.SemaphoreType.DMA((3, CHUNKS)),
        ],
        compiler_params=pltpu.CompilerParams(
            collective_id=0, has_side_effects=True, vmem_limit_bytes=60 * 2 ** 20),
        name="attend_project_migrate",
    )(
        lengths,
        queries.reshape(rows, HD),
        keys.reshape(TOK, HD),
        values.reshape(TOK, HD),
        prior_kv.reshape(512, 2 * HD),
        routes.reshape(1, 32),
        out_weight,
    )
    projected, migrated = pl.pallas_call(
        hand_over,
        out_shape=(
            jax.ShapeDtypeStruct(projected.shape, BF16),
            jax.ShapeDtypeStruct(migrated.shape, BF16),
        ),
        in_specs=[vmem, vmem],
        out_specs=(hbm, hbm),
        scratch_shapes=[pltpu.SemaphoreType.DMA((2,))],
        name="hand_over",
    )(projected, migrated)
    return projected, migrated.reshape(64, BLOCK, 1, 2 * HD)


def solution(mesh):
    placed = (
        P("inst", "head", None),
        P("inst", "head", None),
        P("inst", "head", None),
        P(),
        P("inst", "head", None),
        P("inst", None),
        P("head", None),
    )
    return jax.shard_map(
        shards,
        mesh=mesh,
        in_specs=placed,
        out_specs=(P(("inst", "head"), None), P("inst", None, "head", None)),
        check_vma=False,
    )
```

```python
import functools
import math

import jax
import jax.numpy as jnp
from jax import lax
from jax.experimental import pallas as pl
from jax.experimental.pallas import tpu as pltpu
from jax.sharding import PartitionSpec as P

MESH = pl.DeviceIdType.MESH
F32, BF16 = jnp.float32, jnp.bfloat16
BLOCK = 16
TOK = 256
HEADS = 8
HD = 128
N_INST = 32
WINDOW = 20
GRP = 4
PAD = 4
PARTS = ((0, 96), (96, 64), (160, 96))
QROWS = 512
TILE = 256
CHUNKS = 4
CW = 1024
BIG = float(2 ** 30)
SCALE = math.log2(math.e) / math.sqrt(HD)


def doc_of(positions, ends):
    doc = jnp.zeros(positions.shape, jnp.int32)
    for e in ends:
        doc = doc + (positions >= e).astype(jnp.int32)
    return doc


def kernel(lengths, q_hbm, k_ref, v_ref, prior_hbm, routes, w_hbm,
           out_ref, mig_ref,
           kv, feat, qraw, qf, qx, acc, mx, prior, outgoing, wbuf, att,
           keep, s1_out, s1_in, x_out, x_in, s2_out, s2_in,
           loc, ssem, rsem, msem, mrsem, rs_s, rs_r):
    me = lax.axis_index("inst")
    hd = lax.axis_index("head")
    z, r = me // 8, lax.rem(me, 8)
    y, h = r // 2, lax.rem(r, 2)
    xl, c = hd // 2, lax.rem(hd, 2)
    sib = (me, 2 * xl + 1 - c)
    across = (me, 2 * (1 - xl) + c)

    q_copy = pltpu.make_async_copy(q_hbm, qraw, loc.at[0])
    p_copy = pltpu.make_async_copy(prior_hbm, prior, loc.at[1])
    w_copy = pltpu.make_async_copy(w_hbm, wbuf, loc.at[2])
    q_copy.start()
    p_copy.start()
    w_copy.start()

    barrier = pltpu.get_barrier_semaphore()

    def greet(d, carry):
        pl.semaphore_signal(barrier, inc=1, device_id=(lax.rem(me + d, N_INST), hd), device_id_type=MESH)
        return carry

    lax.fori_loop(1, N_INST, greet, 0)
    pl.semaphore_signal(barrier, inc=1, device_id=sib, device_id_type=MESH)
    pl.semaphore_signal(barrier, inc=1, device_id=across, device_id_type=MESH)

    own = pl.multiple_of((me + PAD) * TOK, TOK)
    kv[pl.ds(own, TOK), :HD] = k_ref[...]
    kv[pl.ds(own, TOK), HD:] = v_ref[...]
    pl.semaphore_wait(barrier, N_INST + 1)

    def piece(part, blk):
        first, rows = PARTS[part]
        return kv.at[pl.ds(pl.multiple_of((blk + PAD) * TOK + first, 16), rows), :]

    def send(part, blk, target, slot):
        return pltpu.make_async_remote_copy(
            src_ref=piece(part, blk), dst_ref=piece(part, blk),
            send_sem=ssem.at[part, slot], recv_sem=rsem.at[part, blk],
            device_id=(target, hd), device_id_type=MESH)

    def arrive(part, blk):
        send(part, blk, me, 0).wait_recv()

    def needs(dst, src):
        return (dst - src >= 1) & (dst - src <= WINDOW)

    def p0_h(act):
        act(send(0, me, z * 8 + y * 2 + 1 - h, 0))

    def p0_y(h1, slot, act):
        def one(n, carry):
            y2 = lax.rem(y + 1 + n, 4)
            @pl.when((z < 3) | (y2 * 2 + h > y * 2 + h1))
            def _():
                act(send(0, z * 8 + y * 2 + h1, z * 8 + y2 * 2 + h, slot + n))
            return carry
        lax.fori_loop(0, 3, one, 0)

    def p0_z(r1, slot, act):
        def one(dz, carry):
            src, dst = z * 8 + r1, me + 8 * dz
            @pl.when((z + dz < 4) & needs(dst, src))
            def _():
                act(send(0, src, dst, slot + dz))
            return carry
        lax.fori_loop(1, 4, one, 0)

    def p0_rest(dz, act):
        def one(n, carry):
            src, dst = z * 8 + lax.rem(y + 1 + n // 2, 4) * 2 + lax.rem(n, 2), me + 8 * dz
            @pl.when((z + dz < 4) & needs(dst, src))
            def _():
                act(send(0, src, dst, 16 + dz * 6 + n))
            return carry
        lax.fori_loop(0, 6, one, 0)

    def p0_plane():
        def one(n, carry):
            r1 = lax.rem(y + 1 + n // 2, 4) * 2 + lax.rem(n, 2)
            @pl.when((z < 3) | (r > r1))
            def _():
                arrive(0, z * 8 + r1)
            return carry
        lax.fori_loop(0, 6, one, 0)

    def column(dz):
        return (z >= dz) & ((dz < 3) | (r >= 4))

    def p12_z(part, act):
        def one(dz, carry):
            @pl.when((z + dz < 4) & ((dz < 3) | (r >= 4)))
            def _():
                act(send(part, me, me + 8 * dz, dz - 1))
            return carry
        lax.fori_loop(1, 4, one, 0)

    def p1_h(dz, act):
        @pl.when(column(dz))
        def _():
            act(send(1, me - 8 * dz, z * 8 + y * 2 + 1 - h, 3 + dz))

    def p1_y(dz, h1, slot, act):
        def one(n, carry):
            src, dst = (z - dz) * 8 + y * 2 + h1, z * 8 + lax.rem(y + 1 + n, 4) * 2 + h
            @pl.when((z >= dz) & needs(dst, src))
            def _():
                act(send(1, src, dst, slot + 6 * dz + n))
            return carry
        lax.fori_loop(0, 3, one, 0)

    def y_wants(dz, r1, y1, y2):
        if dz == 0:
            return y2 > y1
        return (z >= dz) & ((dz == 1) | (r1 >= 2 * y2 + (4 if dz == 3 else -4)))

    def p2_y(dz, act):
        def one(n, carry):
            y2 = lax.rem(y + 1 + n, 4)
            @pl.when(y_wants(dz, r, y, y2))
            def _():
                act(send(2, me - 8 * dz, z * 8 + y2 * 2 + h, 3 + dz * 3 + n))
            return carry
        lax.fori_loop(0, 3, one, 0)

    def p2_h(dz, first, count, slot, act):
        def one(n, carry):
            src = (z - dz) * 8 + lax.rem(y + first + n, 4) * 2 + h
            dst = z * 8 + y * 2 + 1 - h
            @pl.when((z >= dz) & needs(dst, src))
            def _():
                act(send(2, src, dst, slot + dz * 4 + n))
            return carry
        lax.fori_loop(0, count, one, 0)

    def stage0(act):
        p0_h(act)
        p12_z(2, act)
        p12_z(1, act)
        p2_y(0, act)
        p0_y(h, 1, act)
        p1_h(0, act)
        p1_y(0, h, 8, act)
        p2_h(0, 0, 1, 16, act)
        p0_z(r, 6, act)

    def stage1(act, wait):
        if wait:
            arrive(0, z * 8 + y * 2 + 1 - h)
        p0_y(1 - h, 4, act)
        p0_z(y * 2 + 1 - h, 9, act)
        if wait:
            arrive(1, z * 8 + y * 2 + 1 - h)
        p1_y(0, 1 - h, 11, act)
        if wait:
            from_y(0)
        p2_h(0, 1, 3, 17, act)

    def from_y(dz):
        def one(n, carry):
            y1 = lax.rem(y + 1 + n, 4)
            @pl.when(y_wants(dz, y1 * 2 + h, y1, y))
            def _():
                arrive(2, (z - dz) * 8 + y1 * 2 + h)
            return carry
        lax.fori_loop(0, 3, one, 0)

    def stage2(dz, act, wait):
        if wait:
            @pl.when(column(dz))
            def _():
                arrive(2, me - 8 * dz)
                arrive(1, me - 8 * dz)
        p2_y(dz, act)
        p1_h(dz, act)
        p1_y(dz, h, 8, act)
        p2_h(dz, 0, 1, 16, act)

    def stage3(act, wait):
        if wait:
            p0_plane()
        for dz in (1, 2, 3):
            p0_rest(dz, act)

    def stage4(dz, act, wait):
        if wait:
            @pl.when(column(dz))
            def _():
                arrive(1, (z - dz) * 8 + y * 2 + 1 - h)
        p1_y(dz, 1 - h, 11, act)
        if wait:
            from_y(dz)
        p2_h(dz, 1, 3, 17, act)

    start = lambda copy: copy.start()
    done = lambda copy: copy.wait_send()

    stage0(start)

    ends = []
    total = jnp.int32(0)
    for i in range(4):
        total = total + lengths[i]
        ends.append(total)
    kv[: PAD * TOK, :] = jnp.zeros((PAD * TOK, 2 * HD), BF16)

    def key_feature(b, carry):
        pos = (b - PAD) * TOK + lax.broadcasted_iota(jnp.int32, (TOK, HD), 0)
        lane = lax.broadcasted_iota(jnp.int32, (TOK, HD), 1)
        doc = jnp.where(pos < 0, 4, doc_of(pos, ends))
        feat[pl.ds(pl.multiple_of(b * TOK, TOK), TOK), :] = jnp.where(doc == lane, 1.0, 0.0).astype(BF16)
        return carry

    lax.fori_loop(0, N_INST + PAD, key_feature, 0)

    q_copy.wait()

    def widen(t, carry):
        rows = pl.ds(pl.multiple_of(t * TILE, TILE), TILE)
        qf[rows, :] = qraw[rows, :].astype(F32)
        return carry

    lax.fori_loop(0, 8, widen, 0)
    for quarter in range(4):
        pos = me * TOK + quarter * 64 + lax.broadcasted_iota(jnp.int32, (64, HD), 0)
        lane = lax.broadcasted_iota(jnp.int32, (64, HD), 1)
        doc = doc_of(pos, ends)
        mask = jnp.where((lane < 5) & (lane != doc), -BIG, 0.0).astype(BF16)
        for head in range(HEADS):
            rows = slice(quarter * QROWS + head * 64, quarter * QROWS + head * 64 + 64)
            qx[rows, :HD] = qf[pl.ds(quarter * QROWS + head, 64, stride=HEADS), :].astype(BF16)
            qx[rows, HD:] = mask

    def tiles(body, half, count):
        for t in range(count):
            body(pl.multiple_of(half * 1024 + t * TILE, TILE), t)

    ones = jnp.ones((TOK, HD), BF16)

    def diagonal(half, carry):
        def body(base, t):
            rows = pl.ds(base, TILE)
            k = jnp.concatenate([kv[pl.ds(own, TOK), :HD], feat[pl.ds(own, TOK), :]], axis=1)
            v = jnp.concatenate([kv[pl.ds(own, TOK), HD:], ones], axis=1)
            s = lax.dot_general(qx[rows, :], k, (((1,), (1,)), ((), ())), preferred_element_type=F32)
            tok = 128 * half + 64 * (t // 2) + lax.rem(lax.broadcasted_iota(jnp.int32, (TILE, TOK), 0), 64)
            s = jnp.where(lax.broadcasted_iota(jnp.int32, (TILE, TOK), 1) <= tok, s, -BIG)
            m = jnp.broadcast_to(jnp.max(s, axis=1, keepdims=True), (TILE, HD))
            p = jnp.concatenate(
                [jnp.exp2((s[:, j * HD:(j + 1) * HD] - m) * SCALE).astype(BF16) for j in range(TOK // HD)], axis=1)
            mx[rows, :] = m
            acc[rows, :] = jnp.dot(p, v, preferred_element_type=F32)
        tiles(body, half, 4)
        return carry


    def slot_rows(ref, i):
        return ref.at[pl.ds(pl.multiple_of(i * 32, 32), 32), :]

    def migrate(d):
        there = lax.rem(me + d, N_INST)
        return pltpu.make_async_remote_copy(
            src_ref=slot_rows(outgoing, there), dst_ref=slot_rows(mig_ref, me),
            send_sem=msem.at[d], recv_sem=mrsem.at[d], device_id=(there, hd), device_id_type=MESH)

    stay = pltpu.make_async_copy(slot_rows(outgoing, me), slot_rows(mig_ref, me), loc.at[3])

    def collect(g):
        def one(n, carry):
            src = me - 1 - g * GRP - n
            rs = lax.rem(src, 8)
            @pl.when(src >= 0)
            def _():
                @pl.when(src // 8 < z)
                def _():
                    arrive(0, src)
                @pl.when(rs // 2 != y)
                def _():
                    arrive(1, src)
                @pl.when(lax.rem(rs, 2) != h)
                def _():
                    arrive(2, src)
            return carry
        lax.fori_loop(0, GRP, one, 0)

    keys = GRP * TOK
    many = jnp.ones((keys, HD), BF16)

    def attend(g, first_tile, count):
        @pl.when(me - 1 - g * GRP >= 0)
        def _():
            ks = pl.ds(pl.multiple_of((me - g * GRP - GRP + PAD) * TOK, TOK), keys)
            for t in range(count):
                rows = pl.ds(pl.multiple_of(first_tile * TILE + t * TILE, TILE), TILE)
                k = jnp.concatenate([kv[ks, :HD], feat[ks, :]], axis=1)
                s = lax.dot_general(qx[rows, :], k, (((1,), (1,)), ((), ())), preferred_element_type=F32)
                old = mx[rows, :]
                m = jnp.maximum(old, jnp.max(s, axis=1, keepdims=True))
                shrink = jnp.exp2((old - m) * SCALE)
                mx[rows, :] = m
                p = jnp.concatenate(
                    [jnp.exp2((s[:, j * HD:(j + 1) * HD] - m) * SCALE).astype(BF16) for j in range(keys // HD)], axis=1)
                v = jnp.concatenate([kv[ks, HD:], many], axis=1)
                u = jnp.dot(p, v, preferred_element_type=F32)
                a = acc[rows, :]
                acc[rows, :] = jnp.concatenate([a[:, :HD] * shrink, a[:, HD:] * shrink], axis=1) + u

    def full_loop(g, carry):
        collect(g)
        attend(g, 0, 8)
        return carry

    def first_loop(g, carry):
        collect(g)
        attend(g, (1 - xl) * 4, 4)
        return carry

    def second_loop(g, carry):
        attend(g, xl * 4, 4)
        return carry

    def lay_out():
        p_copy.wait()
        row = lax.broadcasted_iota(jnp.int32, (32, 32), 0)
        lane = lax.broadcasted_iota(jnp.int32, (32, 32), 1)
        target = jnp.broadcast_to(routes[...], (32, 32))
        same = jnp.sum(jnp.where(row == lane, target, 0).astype(F32), axis=1, keepdims=True).astype(jnp.int32) == target
        rank = jnp.sum(jnp.where(same & (row < lane), 1.0, 0.0), axis=0, keepdims=True)
        slot = (2 * target[:8]).astype(F32) + jnp.broadcast_to(rank, (8, 32))
        blk = lax.broadcasted_iota(jnp.int32, (32, 512), 0)
        col = lax.broadcasted_iota(jnp.int32, (32, 512), 1)
        spread = jnp.where(blk == col // BLOCK, 1.0, 0.0).astype(BF16)
        slots = jnp.dot(slot.astype(BF16), spread, preferred_element_type=F32)
        code = (slots[:1].astype(jnp.int32)) * BLOCK + lax.rem(col[:1], BLOCK)

        def place(t, carry):
            rows = t * TILE + lax.broadcasted_iota(jnp.int32, (TILE, 512), 0)
            hit = jnp.where(rows == jnp.broadcast_to(code, (TILE, 512)), 1.0, 0.0).astype(BF16)
            outgoing[pl.ds(pl.multiple_of(t * TILE, TILE), TILE), :] = jnp.dot(
                hit, prior[...], preferred_element_type=F32).astype(BF16)
            return carry

        lax.fori_loop(0, 4, place, 0)

    def go(d, carry):
        migrate(d).start()
        return carry

    stage1(start, True)
    stage2(1, start, True)
    stage2(2, start, True)
    p0_plane()
    p0_rest(1, start)
    p0_rest(2, start)
    stage2(3, start, True)
    p0_rest(3, start)
    stage4(1, start, True)
    lax.fori_loop(0, 2, diagonal, 0)
    lay_out()
    stage4(2, start, True)
    stage4(3, start, True)
    lax.fori_loop(0, 2, full_loop, 0)
    stay.start()
    lax.fori_loop(1, N_INST, go, 0)
    lax.fori_loop(2, 5, first_loop, 0)

    def finish(half):
        for which in range(2):
            quarter = half * 2 + (1 - c if which == 0 else c)
            for head in range(HEADS):
                rows = pl.ds(pl.multiple_of(quarter * QROWS + head * 64, 64), 64)
                a = acc[rows, :]
                att[which * 64:(which + 1) * 64, head * HD:(head + 1) * HD] = (a[:, :HD] / a[:, HD:]).astype(BF16)

    def hop(src, dst, n, slot, target):
        return pltpu.make_async_remote_copy(
            src_ref=src.at[n], dst_ref=dst.at[n], send_sem=rs_s.at[slot, n], recv_sem=rs_r.at[slot, n],
            device_id=target, device_id_type=MESH)

    def project(n):
        return jnp.dot(att[...], wbuf[:, pl.ds(pl.multiple_of(n * CW, CW), CW)], preferred_element_type=F32)

    finish(1 - xl)
    w_copy.wait()

    def merge(n):
        hop(s1_out, s1_in, n, 0, sib).wait_recv()
        x_out[n] = (keep[n] + s1_in[n].astype(F32)).astype(BF16)
        hop(x_out, x_in, n, 1, across).start()

    def first_half(n, carry):
        p = project(n)
        s1_out[n] = p[:64].astype(BF16)
        hop(s1_out, s1_in, n, 0, sib).start()
        keep[n] = p[64:]
        @pl.when(n >= 1)
        def _():
            merge(n - 1)
        return carry

    lax.fori_loop(0, CHUNKS, first_half, 0)
    merge(CHUNKS - 1)

    lax.fori_loop(2, 5, second_loop, 0)

    finish(xl)

    def second_half(n, carry):
        p = project(n)
        s2_out[n] = p[:64].astype(BF16)
        hop(s2_out, s2_in, n, 2, sib).start()
        keep[n] = p[64:]
        return carry

    lax.fori_loop(0, CHUNKS, second_half, 0)

    stage0(done)
    stage1(done, False)
    stage3(done, False)
    for dz in (1, 2, 3):
        stage2(dz, done, False)
        stage4(dz, done, False)
    stay.wait()

    def gone(d, carry):
        migrate(d).wait()
        return carry

    lax.fori_loop(1, N_INST, gone, 0)

    def last(n, carry):
        hop(s2_out, s2_in, n, 2, sib).wait_recv()
        hop(x_out, x_in, n, 1, across).wait_recv()
        out_ref[:, pl.ds(pl.multiple_of(n * CW, CW), CW)] = (
            keep[n] + s2_in[n].astype(F32) + x_in[n].astype(F32)).astype(BF16)
        return carry

    lax.fori_loop(0, CHUNKS, last, 0)

    def sent(n, carry):
        hop(s1_out, s1_in, n, 0, sib).wait_send()
        hop(x_out, x_in, n, 1, across).wait_send()
        hop(s2_out, s2_in, n, 2, sib).wait_send()
        return carry

    lax.fori_loop(0, CHUNKS, sent, 0)


def hand_over(a, b, a_out, b_out, sem):
    first = pltpu.make_async_copy(a, a_out, sem.at[0])
    second = pltpu.make_async_copy(b, b_out, sem.at[1])
    first.start()
    second.start()
    first.wait()
    second.wait()


def shards(queries, keys, values, lengths, prior_kv, routes, out_weight):
    rows = TOK * HEADS
    vmem = pl.BlockSpec(memory_space=pltpu.VMEM)
    hbm = pl.BlockSpec(memory_space=pl.ANY)
    blocks = (PAD + N_INST) * TOK
    quarter = (CHUNKS, 64, CW)
    projected, migrated = pl.pallas_call(
        kernel,
        out_shape=(
            jax.ShapeDtypeStruct((64, CHUNKS * CW), BF16),
            jax.ShapeDtypeStruct((N_INST * 2 * BLOCK, 2 * HD), BF16),
        ),
        in_specs=[pl.BlockSpec(memory_space=pltpu.SMEM), hbm, vmem, vmem, hbm, vmem, hbm],
        out_specs=(vmem, hbm),
        scratch_shapes=[
            pltpu.VMEM((blocks, 2 * HD), BF16),
            pltpu.VMEM((blocks, HD), BF16),
            pltpu.VMEM((rows, HD), BF16),
            pltpu.VMEM((rows, HD), F32),
            pltpu.VMEM((rows, 2 * HD), BF16),
            pltpu.VMEM((rows, 2 * HD), F32),
            pltpu.VMEM((rows, HD), F32),
            pltpu.VMEM((512, 2 * HD), BF16),
            pltpu.VMEM((1024, 2 * HD), BF16),
            pltpu.VMEM((HEADS * HD, CHUNKS * CW), BF16),
            pltpu.VMEM((128, HEADS * HD), BF16),
            pltpu.VMEM(quarter, F32),
            pltpu.VMEM(quarter, BF16),
            pltpu.VMEM(quarter, BF16),
            pltpu.VMEM(quarter, BF16),
            pltpu.VMEM(quarter, BF16),
            pltpu.VMEM(quarter, BF16),
            pltpu.VMEM(quarter, BF16),
            pltpu.SemaphoreType.DMA((4,)),
            pltpu.SemaphoreType.DMA((3, 48)),
            pltpu.SemaphoreType.DMA((3, 48)),
            pltpu.SemaphoreType.DMA((32,)),
            pltpu.SemaphoreType.DMA((32,)),
            pltpu.SemaphoreType.DMA((3, CHUNKS)),
            pltpu.SemaphoreType.DMA((3, CHUNKS)),
        ],
        compiler_params=pltpu.CompilerParams(
            collective_id=0, has_side_effects=True, vmem_limit_bytes=60 * 2 ** 20),
        name="attend_project_migrate",
    )(
        lengths,
        queries.reshape(rows, HD),
        keys.reshape(TOK, HD),
        values.reshape(TOK, HD),
        prior_kv.reshape(512, 2 * HD),
        routes.reshape(1, 32),
        out_weight,
    )
    projected, migrated = pl.pallas_call(
        hand_over,
        out_shape=(
            jax.ShapeDtypeStruct(projected.shape, BF16),
            jax.ShapeDtypeStruct(migrated.shape, BF16),
        ),
        in_specs=[vmem, vmem],
        out_specs=(hbm, hbm),
        scratch_shapes=[pltpu.SemaphoreType.DMA((2,))],
        name="hand_over",
    )(projected, migrated)
    return projected, migrated.reshape(64, BLOCK, 1, 2 * HD)


def solution(mesh):
    placed = (
        P("inst", "head", None),
        P("inst", "head", None),
        P("inst", "head", None),
        P(),
        P("inst", "head", None),
        P("inst", None),
        P("head", None),
    )
    return jax.shard_map(
        shards,
        mesh=mesh,
        in_specs=placed,
        out_specs=(P(("inst", "head"), None), P("inst", None, "head", None)),
        check_vma=False,
    )
```

```python
import functools
import math

import jax
import jax.numpy as jnp
from jax import lax
from jax.experimental import pallas as pl
from jax.experimental.pallas import tpu as pltpu
from jax.sharding import PartitionSpec as P

MESH = pl.DeviceIdType.MESH
F32, BF16 = jnp.float32, jnp.bfloat16
BLOCK = 16
TOK = 256
HEADS = 8
HD = 128
N_INST = 32
WINDOW = 20
GRP = 4
PAD = 4
PARTS = ((0, 96), (96, 64), (160, 96))
QROWS = 512
TILE = 256
CHUNKS = 4
PIECES = 4
CW = 1024
BIG = float(2 ** 30)
SCALE = math.log2(math.e) / math.sqrt(HD)


def doc_of(positions, ends):
    doc = jnp.zeros(positions.shape, jnp.int32)
    for e in ends:
        doc = doc + (positions >= e).astype(jnp.int32)
    return doc


def kernel(lengths, q_hbm, k_ref, v_ref, prior_hbm, routes, w_hbm,
           out_ref, mig_ref,
           kv, feat, qraw, qf, qx, acc, mx, prior, outgoing, wbuf, att,
           keep, s1_out, s1_in, x_out, x_in, s2_out, s2_in,
           loc, ssem, rsem, msem, mrsem, rs_s, rs_r):
    me = lax.axis_index("inst")
    hd = lax.axis_index("head")
    z, r = me // 8, lax.rem(me, 8)
    y, h = r // 2, lax.rem(r, 2)
    xl, c = hd // 2, lax.rem(hd, 2)
    sib = (me, 2 * xl + 1 - c)
    across = (me, 2 * (1 - xl) + c)

    q_copy = pltpu.make_async_copy(q_hbm, qraw, loc.at[0])
    p_copy = pltpu.make_async_copy(prior_hbm, prior, loc.at[1])
    w_copy = pltpu.make_async_copy(w_hbm, wbuf, loc.at[2])
    q_copy.start()
    p_copy.start()
    w_copy.start()

    barrier = pltpu.get_barrier_semaphore()

    def greet(d, carry):
        pl.semaphore_signal(barrier, inc=1, device_id=(lax.rem(me + d, N_INST), hd), device_id_type=MESH)
        return carry

    lax.fori_loop(1, N_INST, greet, 0)
    pl.semaphore_signal(barrier, inc=1, device_id=sib, device_id_type=MESH)
    pl.semaphore_signal(barrier, inc=1, device_id=across, device_id_type=MESH)

    own = pl.multiple_of((me + PAD) * TOK, TOK)
    kv[pl.ds(own, TOK), :HD] = k_ref[...]
    kv[pl.ds(own, TOK), HD:] = v_ref[...]
    pl.semaphore_wait(barrier, N_INST + 1)

    def piece(part, blk):
        first, rows = PARTS[part]
        return kv.at[pl.ds(pl.multiple_of((blk + PAD) * TOK + first, 16), rows), :]

    def send(part, blk, target, slot):
        return pltpu.make_async_remote_copy(
            src_ref=piece(part, blk), dst_ref=piece(part, blk),
            send_sem=ssem.at[part, slot], recv_sem=rsem.at[part, blk],
            device_id=(target, hd), device_id_type=MESH)

    def arrive(part, blk):
        send(part, blk, me, 0).wait_recv()

    def needs(dst, src):
        return (dst - src >= 1) & (dst - src <= WINDOW)

    def p0_h(act):
        act(send(0, me, z * 8 + y * 2 + 1 - h, 0))

    def p0_y(h1, slot, act):
        def one(n, carry):
            y2 = lax.rem(y + 1 + n, 4)
            @pl.when((z < 3) | (y2 * 2 + h > y * 2 + h1))
            def _():
                act(send(0, z * 8 + y * 2 + h1, z * 8 + y2 * 2 + h, slot + n))
            return carry
        lax.fori_loop(0, 3, one, 0)

    def p0_z(r1, slot, act):
        def one(dz, carry):
            src, dst = z * 8 + r1, me + 8 * dz
            @pl.when((z + dz < 4) & needs(dst, src))
            def _():
                act(send(0, src, dst, slot + dz))
            return carry
        lax.fori_loop(1, 4, one, 0)

    def p0_rest(dz, act):
        def one(n, carry):
            src, dst = z * 8 + lax.rem(y + 1 + n // 2, 4) * 2 + lax.rem(n, 2), me + 8 * dz
            @pl.when((z + dz < 4) & needs(dst, src))
            def _():
                act(send(0, src, dst, 16 + dz * 6 + n))
            return carry
        lax.fori_loop(0, 6, one, 0)

    def p0_plane():
        def one(n, carry):
            r1 = lax.rem(y + 1 + n // 2, 4) * 2 + lax.rem(n, 2)
            @pl.when((z < 3) | (r > r1))
            def _():
                arrive(0, z * 8 + r1)
            return carry
        lax.fori_loop(0, 6, one, 0)

    def column(dz):
        return (z >= dz) & ((dz < 3) | (r >= 4))

    def p12_z(part, act):
        def one(dz, carry):
            @pl.when((z + dz < 4) & ((dz < 3) | (r >= 4)))
            def _():
                act(send(part, me, me + 8 * dz, dz - 1))
            return carry
        lax.fori_loop(1, 4, one, 0)

    def p1_h(dz, act):
        @pl.when(column(dz))
        def _():
            act(send(1, me - 8 * dz, z * 8 + y * 2 + 1 - h, 3 + dz))

    def p1_y(dz, h1, slot, act):
        def one(n, carry):
            src, dst = (z - dz) * 8 + y * 2 + h1, z * 8 + lax.rem(y + 1 + n, 4) * 2 + h
            @pl.when((z >= dz) & needs(dst, src))
            def _():
                act(send(1, src, dst, slot + 6 * dz + n))
            return carry
        lax.fori_loop(0, 3, one, 0)

    def y_wants(dz, r1, y1, y2):
        if dz == 0:
            return y2 > y1
        return (z >= dz) & ((dz == 1) | (r1 >= 2 * y2 + (4 if dz == 3 else -4)))

    def p2_y(dz, act):
        def one(n, carry):
            y2 = lax.rem(y + 1 + n, 4)
            @pl.when(y_wants(dz, r, y, y2))
            def _():
                act(send(2, me - 8 * dz, z * 8 + y2 * 2 + h, 3 + dz * 3 + n))
            return carry
        lax.fori_loop(0, 3, one, 0)

    def p2_h(dz, first, count, slot, act):
        def one(n, carry):
            src = (z - dz) * 8 + lax.rem(y + first + n, 4) * 2 + h
            dst = z * 8 + y * 2 + 1 - h
            @pl.when((z >= dz) & needs(dst, src))
            def _():
                act(send(2, src, dst, slot + dz * 4 + n))
            return carry
        lax.fori_loop(0, count, one, 0)

    def stage0(act):
        p0_h(act)
        p12_z(2, act)
        p12_z(1, act)
        p2_y(0, act)
        p0_y(h, 1, act)
        p1_h(0, act)
        p1_y(0, h, 8, act)
        p2_h(0, 0, 1, 16, act)
        p0_z(r, 6, act)

    def stage1(act, wait):
        if wait:
            arrive(0, z * 8 + y * 2 + 1 - h)
        p0_y(1 - h, 4, act)
        p0_z(y * 2 + 1 - h, 9, act)
        if wait:
            arrive(1, z * 8 + y * 2 + 1 - h)
        p1_y(0, 1 - h, 11, act)
        if wait:
            from_y(0)
        p2_h(0, 1, 3, 17, act)

    def from_y(dz):
        def one(n, carry):
            y1 = lax.rem(y + 1 + n, 4)
            @pl.when(y_wants(dz, y1 * 2 + h, y1, y))
            def _():
                arrive(2, (z - dz) * 8 + y1 * 2 + h)
            return carry
        lax.fori_loop(0, 3, one, 0)

    def stage2(dz, act, wait):
        if wait:
            @pl.when(column(dz))
            def _():
                arrive(2, me - 8 * dz)
                arrive(1, me - 8 * dz)
        p2_y(dz, act)
        p1_h(dz, act)
        p1_y(dz, h, 8, act)
        p2_h(dz, 0, 1, 16, act)

    def stage3(act, wait):
        if wait:
            p0_plane()
        for dz in (1, 2, 3):
            p0_rest(dz, act)

    def stage4(dz, act, wait):
        if wait:
            @pl.when(column(dz))
            def _():
                arrive(1, (z - dz) * 8 + y * 2 + 1 - h)
        p1_y(dz, 1 - h, 11, act)
        if wait:
            from_y(dz)
        p2_h(dz, 1, 3, 17, act)

    start = lambda copy: copy.start()
    done = lambda copy: copy.wait_send()

    stage0(start)

    ends = []
    total = jnp.int32(0)
    for i in range(4):
        total = total + lengths[i]
        ends.append(total)
    kv[: PAD * TOK, :] = jnp.zeros((PAD * TOK, 2 * HD), BF16)

    def key_feature(b, carry):
        pos = (b - PAD) * TOK + lax.broadcasted_iota(jnp.int32, (TOK, HD), 0)
        lane = lax.broadcasted_iota(jnp.int32, (TOK, HD), 1)
        doc = jnp.where(pos < 0, 4, doc_of(pos, ends))
        feat[pl.ds(pl.multiple_of(b * TOK, TOK), TOK), :] = jnp.where(doc == lane, 1.0, 0.0).astype(BF16)
        return carry

    lax.fori_loop(0, N_INST + PAD, key_feature, 0)

    q_copy.wait()

    def widen(t, carry):
        rows = pl.ds(pl.multiple_of(t * TILE, TILE), TILE)
        qf[rows, :] = qraw[rows, :].astype(F32)
        return carry

    lax.fori_loop(0, 8, widen, 0)
    for quarter in range(4):
        pos = me * TOK + quarter * 64 + lax.broadcasted_iota(jnp.int32, (64, HD), 0)
        lane = lax.broadcasted_iota(jnp.int32, (64, HD), 1)
        doc = doc_of(pos, ends)
        mask = jnp.where((lane < 5) & (lane != doc), -BIG, 0.0).astype(BF16)
        for head in range(HEADS):
            rows = slice(quarter * QROWS + head * 64, quarter * QROWS + head * 64 + 64)
            qx[rows, :HD] = qf[pl.ds(quarter * QROWS + head, 64, stride=HEADS), :].astype(BF16)
            qx[rows, HD:] = mask

    def tiles(body, half, count):
        for t in range(count):
            body(pl.multiple_of(half * 1024 + t * TILE, TILE), t)

    ones = jnp.ones((TOK, HD), BF16)

    def diagonal(half, carry):
        def body(base, t):
            rows = pl.ds(base, TILE)
            k = jnp.concatenate([kv[pl.ds(own, TOK), :HD], feat[pl.ds(own, TOK), :]], axis=1)
            v = jnp.concatenate([kv[pl.ds(own, TOK), HD:], ones], axis=1)
            s = lax.dot_general(qx[rows, :], k, (((1,), (1,)), ((), ())), preferred_element_type=F32)
            tok = 128 * half + 64 * (t // 2) + lax.rem(lax.broadcasted_iota(jnp.int32, (TILE, TOK), 0), 64)
            s = jnp.where(lax.broadcasted_iota(jnp.int32, (TILE, TOK), 1) <= tok, s, -BIG)
            m = jnp.broadcast_to(jnp.max(s, axis=1, keepdims=True), (TILE, HD))
            p = jnp.concatenate(
                [jnp.exp2((s[:, j * HD:(j + 1) * HD] - m) * SCALE).astype(BF16) for j in range(TOK // HD)], axis=1)
            mx[rows, :] = m
            acc[rows, :] = jnp.dot(p, v, preferred_element_type=F32)
        tiles(body, half, 4)
        return carry


    def slot_rows(ref, i):
        return ref.at[pl.ds(pl.multiple_of(i * 32, 32), 32), :]

    def migrate(d):
        there = lax.rem(me + d, N_INST)
        return pltpu.make_async_remote_copy(
            src_ref=slot_rows(outgoing, there), dst_ref=slot_rows(mig_ref, me),
            send_sem=msem.at[d], recv_sem=mrsem.at[d], device_id=(there, hd), device_id_type=MESH)

    stay = pltpu.make_async_copy(slot_rows(outgoing, me), slot_rows(mig_ref, me), loc.at[3])

    def collect(g):
        def one(n, carry):
            src = me - 1 - g * GRP - n
            rs = lax.rem(src, 8)
            @pl.when(src >= 0)
            def _():
                @pl.when(src // 8 < z)
                def _():
                    arrive(0, src)
                @pl.when(rs // 2 != y)
                def _():
                    arrive(1, src)
                @pl.when(lax.rem(rs, 2) != h)
                def _():
                    arrive(2, src)
            return carry
        lax.fori_loop(0, GRP, one, 0)

    keys = GRP * TOK
    many = jnp.ones((keys, HD), BF16)

    def attend(g, first_tile, count):
        @pl.when(me - 1 - g * GRP >= 0)
        def _():
            ks = pl.ds(pl.multiple_of((me - g * GRP - GRP + PAD) * TOK, TOK), keys)
            for t in range(count):
                rows = pl.ds(pl.multiple_of(first_tile * TILE + t * TILE, TILE), TILE)
                k = jnp.concatenate([kv[ks, :HD], feat[ks, :]], axis=1)
                s = lax.dot_general(qx[rows, :], k, (((1,), (1,)), ((), ())), preferred_element_type=F32)
                old = mx[rows, :]
                m = jnp.maximum(old, jnp.max(s, axis=1, keepdims=True))
                shrink = jnp.exp2((old - m) * SCALE)
                mx[rows, :] = m
                p = jnp.concatenate(
                    [jnp.exp2((s[:, j * HD:(j + 1) * HD] - m) * SCALE).astype(BF16) for j in range(keys // HD)], axis=1)
                v = jnp.concatenate([kv[ks, HD:], many], axis=1)
                u = jnp.dot(p, v, preferred_element_type=F32)
                a = acc[rows, :]
                acc[rows, :] = jnp.concatenate([a[:, :HD] * shrink, a[:, HD:] * shrink], axis=1) + u

    def full_loop(g, carry):
        collect(g)
        attend(g, 0, 8)
        return carry

    def first_loop(g, carry):
        collect(g)
        attend(g, (1 - xl) * 4, 4)
        return carry

    def second_loop(g, carry):
        attend(g, xl * 4, 4)
        return carry

    def lay_out():
        p_copy.wait()
        row = lax.broadcasted_iota(jnp.int32, (32, 32), 0)
        lane = lax.broadcasted_iota(jnp.int32, (32, 32), 1)
        target = jnp.broadcast_to(routes[...], (32, 32))
        same = jnp.sum(jnp.where(row == lane, target, 0).astype(F32), axis=1, keepdims=True).astype(jnp.int32) == target
        rank = jnp.sum(jnp.where(same & (row < lane), 1.0, 0.0), axis=0, keepdims=True)
        slot = (2 * target[:8]).astype(F32) + jnp.broadcast_to(rank, (8, 32))
        blk = lax.broadcasted_iota(jnp.int32, (32, 512), 0)
        col = lax.broadcasted_iota(jnp.int32, (32, 512), 1)
        spread = jnp.where(blk == col // BLOCK, 1.0, 0.0).astype(BF16)
        slots = jnp.dot(slot.astype(BF16), spread, preferred_element_type=F32)
        code = (slots[:1].astype(jnp.int32)) * BLOCK + lax.rem(col[:1], BLOCK)

        def place(t, carry):
            rows = t * TILE + lax.broadcasted_iota(jnp.int32, (TILE, 512), 0)
            hit = jnp.where(rows == jnp.broadcast_to(code, (TILE, 512)), 1.0, 0.0).astype(BF16)
            outgoing[pl.ds(pl.multiple_of(t * TILE, TILE), TILE), :] = jnp.dot(
                hit, prior[...], preferred_element_type=F32).astype(BF16)
            return carry

        lax.fori_loop(0, 4, place, 0)

    def go(d, carry):
        migrate(d).start()
        return carry

    stage1(start, True)
    stage2(1, start, True)
    stage2(2, start, True)
    p0_plane()
    p0_rest(1, start)
    stage2(3, start, True)
    stage4(1, start, True)
    p0_rest(2, start)
    lax.fori_loop(0, 2, diagonal, 0)
    lay_out()
    p0_rest(3, start)
    stage4(2, start, True)
    stage4(3, start, True)
    lax.fori_loop(0, 2, full_loop, 0)
    stay.start()
    lax.fori_loop(1, N_INST, go, 0)
    lax.fori_loop(2, 5, first_loop, 0)

    def finish(half):
        for which in range(2):
            quarter = half * 2 + (1 - c if which == 0 else c)
            for head in range(HEADS):
                rows = pl.ds(pl.multiple_of(quarter * QROWS + head * 64, 64), 64)
                a = acc[rows, :]
                att[which * 64:(which + 1) * 64, head * HD:(head + 1) * HD] = (a[:, :HD] / a[:, HD:]).astype(BF16)

    def hop(src, dst, n, slot, target):
        return pltpu.make_async_remote_copy(
            src_ref=src.at[n], dst_ref=dst.at[n], send_sem=rs_s.at[slot, n], recv_sem=rs_r.at[slot, n],
            device_id=target, device_id_type=MESH)

    def project(n):
        return jnp.dot(att[...], wbuf[:, pl.ds(pl.multiple_of(n * CW, CW), CW)], preferred_element_type=F32)

    finish(1 - xl)
    w_copy.wait()

    def merge(n):
        hop(s1_out, s1_in, n, 0, sib).wait_recv()
        x_out[n] = (keep[n] + s1_in[n].astype(F32)).astype(BF16)
        hop(x_out, x_in, n, 1, across).start()

    def first_half(n, carry):
        p = project(n)
        s1_out[n] = p[:64].astype(BF16)
        hop(s1_out, s1_in, n, 0, sib).start()
        keep[n] = p[64:]
        @pl.when(n >= 1)
        def _():
            merge(n - 1)
        return carry

    lax.fori_loop(0, CHUNKS, first_half, 0)
    merge(CHUNKS - 1)

    lax.fori_loop(2, 5, second_loop, 0)

    finish(xl)

    def second_half(n, carry):
        p = project(n)
        s2_out[n] = p[:64].astype(BF16)
        hop(s2_out, s2_in, n, 2, sib).start()
        keep[n] = p[64:]
        return carry

    lax.fori_loop(0, CHUNKS, second_half, 0)

    stage0(done)
    stage1(done, False)
    stage3(done, False)
    for dz in (1, 2, 3):
        stage2(dz, done, False)
        stage4(dz, done, False)
    stay.wait()

    def gone(d, carry):
        migrate(d).wait()
        return carry

    lax.fori_loop(1, N_INST, gone, 0)

    def last(n, carry):
        hop(s2_out, s2_in, n, 2, sib).wait_recv()
        hop(x_out, x_in, n, 1, across).wait_recv()
        out_ref[:, pl.ds(pl.multiple_of(n * CW, CW), CW)] = (
            keep[n] + s2_in[n].astype(F32) + x_in[n].astype(F32)).astype(BF16)
        return carry

    lax.fori_loop(0, CHUNKS, last, 0)

    def sent(n, carry):
        hop(s1_out, s1_in, n, 0, sib).wait_send()
        hop(x_out, x_in, n, 1, across).wait_send()
        hop(s2_out, s2_in, n, 2, sib).wait_send()
        return carry

    lax.fori_loop(0, CHUNKS, sent, 0)


def hand_over(a, b, a_out, b_out, a_here, b_here, arrived, left):
    moves = []
    for i, (src, here, dst) in enumerate(((a, a_here, a_out), (b, b_here, b_out))):
        rows = src.shape[0] // PIECES
        for n in range(PIECES):
            part = pl.ds(n * rows, rows)
            moves.append((
                pltpu.make_async_copy(src.at[part, :], here.at[part, :], arrived.at[i, n]),
                pltpu.make_async_copy(here.at[part, :], dst.at[part, :], left.at[i, n])))
    for inward, _ in moves:
        inward.start()
    for inward, outward in moves:
        inward.wait()
        outward.start()
    for _, outward in moves:
        outward.wait()


def shards(queries, keys, values, lengths, prior_kv, routes, out_weight):
    rows = TOK * HEADS
    vmem = pl.BlockSpec(memory_space=pltpu.VMEM)
    hbm = pl.BlockSpec(memory_space=pl.ANY)
    blocks = (PAD + N_INST) * TOK
    quarter = (CHUNKS, 64, CW)
    projected, migrated = pl.pallas_call(
        kernel,
        out_shape=(
            jax.ShapeDtypeStruct((64, CHUNKS * CW), BF16),
            jax.ShapeDtypeStruct((N_INST * 2 * BLOCK, 2 * HD), BF16),
        ),
        in_specs=[pl.BlockSpec(memory_space=pltpu.SMEM), hbm, vmem, vmem, hbm, vmem, hbm],
        out_specs=(vmem, hbm),
        scratch_shapes=[
            pltpu.VMEM((blocks, 2 * HD), BF16),
            pltpu.VMEM((blocks, HD), BF16),
            pltpu.VMEM((rows, HD), BF16),
            pltpu.VMEM((rows, HD), F32),
            pltpu.VMEM((rows, 2 * HD), BF16),
            pltpu.VMEM((rows, 2 * HD), F32),
            pltpu.VMEM((rows, HD), F32),
            pltpu.VMEM((512, 2 * HD), BF16),
            pltpu.VMEM((1024, 2 * HD), BF16),
            pltpu.VMEM((HEADS * HD, CHUNKS * CW), BF16),
            pltpu.VMEM((128, HEADS * HD), BF16),
            pltpu.VMEM(quarter, F32),
            pltpu.VMEM(quarter, BF16),
            pltpu.VMEM(quarter, BF16),
            pltpu.VMEM(quarter, BF16),
            pltpu.VMEM(quarter, BF16),
            pltpu.VMEM(quarter, BF16),
            pltpu.VMEM(quarter, BF16),
            pltpu.SemaphoreType.DMA((4,)),
            pltpu.SemaphoreType.DMA((3, 48)),
            pltpu.SemaphoreType.DMA((3, 48)),
            pltpu.SemaphoreType.DMA((32,)),
            pltpu.SemaphoreType.DMA((32,)),
            pltpu.SemaphoreType.DMA((3, CHUNKS)),
            pltpu.SemaphoreType.DMA((3, CHUNKS)),
        ],
        compiler_params=pltpu.CompilerParams(
            collective_id=0, has_side_effects=True, vmem_limit_bytes=60 * 2 ** 20),
        name="attend_project_migrate",
    )(
        lengths,
        queries.reshape(rows, HD),
        keys.reshape(TOK, HD),
        values.reshape(TOK, HD),
        prior_kv.reshape(512, 2 * HD),
        routes.reshape(1, 32),
        out_weight,
    )
    projected, migrated = pl.pallas_call(
        hand_over,
        out_shape=(
            jax.ShapeDtypeStruct(projected.shape, BF16),
            jax.ShapeDtypeStruct(migrated.shape, BF16),
        ),
        in_specs=[hbm, hbm],
        out_specs=(hbm, hbm),
        scratch_shapes=[
            pltpu.VMEM(projected.shape, BF16),
            pltpu.VMEM(migrated.shape, BF16),
            pltpu.SemaphoreType.DMA((2, PIECES)),
            pltpu.SemaphoreType.DMA((2, PIECES)),
        ],
        name="hand_over",
    )(projected, migrated)
    return projected, migrated.reshape(64, BLOCK, 1, 2 * HD)


def solution(mesh):
    placed = (
        P("inst", "head", None),
        P("inst", "head", None),
        P("inst", "head", None),
        P(),
        P("inst", "head", None),
        P("inst", None),
        P("head", None),
    )
    return jax.shard_map(
        shards,
        mesh=mesh,
        in_specs=placed,
        out_specs=(P(("inst", "head"), None), P("inst", None, "head", None)),
        check_vma=False,
    )
```
